256 devices in a mesh: lat: 16 (over y_hi, x, core), lon: 16 (over z, y_lo).
Axes of the slice: x: 4, y: 4 (y_hi: 2, y_lo: 2; y = y_hi * 2 + y_lo), z: 8, core: 2. Of those that a mesh axis runs over, the one named last changes fastest.
Arguments:
- levels_in: bfloat16 [13, 96, 192, 512], P(None, 'lat', 'lon'), may hold values from -6 to 6
- latent_queries: bfloat16 [2, 512], replicated, may hold values from -6 to 6
- enc_kv: bfloat16 [512, 1024], replicated, may hold values from -0.25 to 0.25
- enc_out: bfloat16 [512, 512], replicated, may hold values from -0.25 to 0.25
- enc_temp: float32 [16], replicated, may hold values from 0.5 to 10
- w_qkv: bfloat16 [512, 1536], replicated, may hold values from -0.25 to 0.25
- w_out: bfloat16 [512, 512], replicated, may hold values from -0.25 to 0.25
- swin_temp: float32 [16], replicated, may hold values from 0.5 to 10
- lat_shift: int32 [1], replicated, may hold values from 1 to 5
- lon_shift: int32 [1], replicated, may hold values from 1 to 11
- key_valid: int32 [96, 192], P('lat', 'lon'), may hold values 0 or 1
- output_grad: bfloat16 [2, 96, 192, 512], P(None, 'lat', 'lon'), may hold values from -6 to 6
Outputs:
- output: bfloat16 [2, 96, 192, 512], P(None, 'lat', 'lon')
- levels_grad: bfloat16 [13, 96, 192, 512], P(None, 'lat', 'lon')
- w_qkv_grad: float32 [786432], P(('lat', 'lon'))
- w_out_grad: float32 [262144], P(('lat', 'lon'))
The draws below stay inside these ranges and needn't reach their ends.
All inputs are finite; a program needn't handle non-finite values. No bound on the sum of `key_valid` on one device may be relied on, other than what follows from the above.
Results may differ from the reference program's by a relative error of at most 0.03.
Values may be sent and summed in bfloat16 or wider, within the bound.
A program may use at most 128 MiB of HBM per device.

```python
import math
import jax
import jax.numpy as jnp
from jax import lax

D = 512
HEADS = 16
LEVELS = 13
LEV = 2
WLAT = 6
WLON = 12
LAT_DEV = 6
NLAT = 96
NLON = 192


def log_spread(key, upper):
    unit = jax.random.uniform(key, (HEADS,), jnp.float32)
    return 0.5 * jnp.exp(unit * math.log(upper / 0.5))


def draw_enc_temp(key, part):
    key = jax.random.fold_in(key, 21)
    upper = 4.0
    return log_spread(key, upper)


def draw_swin_temp(key, part):
    key = jax.random.fold_in(key, 37)
    upper = 4.0
    return log_spread(key, upper)


def set_ends(array, rng, least, largest):
    longest = array.shape.index(max(array.shape))
    spots = []
    for shift in (0, 1):
        where = [jax.random.randint(jax.random.fold_in(rng, axis), (), 0, length) for axis, length in enumerate(array.shape)]
        where[longest] = (where[longest] + shift) % array.shape[longest]
        spots.append(tuple(where))
    return array.at[spots[0]].set(least).at[spots[1]].set(largest)


def level_of(rng, extent, split, low, top_value):
    gain = 1.0
    for position, shards_of in split:
        steps = jax.random.uniform(jax.random.fold_in(jax.random.fold_in(rng, 6), position), (shards_of,), jnp.float32, low / len(split), top_value / len(split))
        gain = gain * jnp.repeat(jnp.exp(steps), extent[position] // shards_of).reshape((-1,) + (1,) * (len(extent) - 1 - position))
    return gain


def gaussian(stream_key, shape, width, reach, cuts=(), held_as=jnp.bfloat16):
    values = jax.random.normal(stream_key, shape, jnp.float32) * width
    if len(cuts) > 0:
        values = level_of(stream_key, shape, cuts, -0.22, 0.18) * values
    return jnp.clip(values, min=-reach, max=reach).astype(held_as)


def setup_inputs(seed: int = 0) -> dict:
    key_list = jax.random.split(jax.random.key(seed), 13)
    levels_in = gaussian(key_list[0], (LEVELS, NLAT, NLON, D), 1.0, 6.0, ((1, 16), (2, 16)))
    latent_queries = gaussian(key_list[1], (LEV, D), 1.0, 6.0)
    enc_kv = gaussian(key_list[2], (D, 2 * D), D ** -0.5, 0.25)
    enc_out = gaussian(key_list[3], (D, D), D ** -0.5, 0.25)
    enc_temp = draw_enc_temp(jax.random.fold_in(key_list[12], 71), 0)
    w_qkv = gaussian(key_list[5], (D, 3 * D), D ** -0.5, 0.25)
    w_out = gaussian(key_list[6], (D, D), D ** -0.5, 0.25)
    swin_temp = draw_swin_temp(jax.random.fold_in(key_list[12], 71), 0)
    lat_shift = jax.random.randint(key_list[8], (1,), 1, WLAT).astype(jnp.int32)
    lon_shift = jax.random.randint(key_list[9], (1,), 1, WLON).astype(jnp.int32)
    key_valid = set_ends((jax.random.randint(key_list[10], (NLAT, NLON), 0, 4) < 3).astype(jnp.int32), jax.random.fold_in(key_list[10], 1), 0, 1)
    output_grad = gaussian(key_list[11], (LEV, NLAT, NLON, D), 1.0, 6.0, ((1, 16), (2, 16)))
    return dict(levels_in=levels_in, latent_queries=latent_queries, enc_kv=enc_kv, enc_out=enc_out, enc_temp=enc_temp, w_qkv=w_qkv, w_out=w_out, swin_temp=swin_temp, lat_shift=lat_shift, lon_shift=lon_shift, key_valid=key_valid, output_grad=output_grad)


EPS = 1e-05
NEG = -1e+30
GRAD_GAIN = 6.0

def narrow(values):
    return lax.optimization_barrier(values.astype(jnp.bfloat16)).astype(jnp.float32)

def layer_norm(values):
    row_mean = lax.optimization_barrier(jnp.mean(values, -1, keepdims=True))
    centered = values - row_mean
    variance = lax.optimization_barrier(jnp.mean(centered * centered, -1, keepdims=True))
    inverse = lax.rsqrt(variance + EPS)
    return (centered * inverse, inverse)

def norm_back(unit, inverse, gradient):
    mean_grad = lax.optimization_barrier(jnp.mean(gradient, -1, keepdims=True))
    mean_cross = lax.optimization_barrier(jnp.mean(gradient * unit, -1, keepdims=True))
    return inverse * (gradient - mean_grad - unit * mean_cross)

def attend(queries, key_part, value_part, allowed, logit_scale):
    scores = jnp.einsum('bqhe,bkhe->bhqk', queries, key_part, precision=lax.Precision.HIGHEST)
    scores = scores * logit_scale[None, :, None, None]
    if allowed is not None:
        scores = jnp.where(allowed[:, None], scores, NEG)
    row_peak = lax.optimization_barrier(jnp.max(scores, -1, keepdims=True))
    exponent = jnp.exp(scores - row_peak)
    probability = exponent / lax.optimization_barrier(jnp.sum(exponent, -1, keepdims=True))
    narrowed = narrow(probability)
    context = jnp.einsum('bhqk,bkhe->bqhe', narrowed, value_part, precision=lax.Precision.HIGHEST)
    return (context, probability, narrowed)

def attend_back(queries, key_part, value_part, probability, narrowed, context_grad, logit_scale):
    prob_grad = jnp.einsum('bqhe,bkhe->bhqk', context_grad, value_part, precision=lax.Precision.HIGHEST)
    value_grad = jnp.einsum('bhqk,bqhe->bkhe', narrowed, context_grad, precision=lax.Precision.HIGHEST)
    score_grad = probability * (prob_grad - lax.optimization_barrier(jnp.sum(probability * prob_grad, -1, keepdims=True)))
    score_grad = score_grad * logit_scale[None, :, None, None]
    query_grad = jnp.einsum('bhqk,bkhe->bqhe', score_grad, key_part, precision=lax.Precision.HIGHEST)
    key_grad = jnp.einsum('bhqk,bqhe->bkhe', score_grad, queries, precision=lax.Precision.HIGHEST)
    return (query_grad, key_grad, value_grad)

def to_windows(field):
    level_count, row_count, col_count, last_dim = field.shape
    shaped = field.reshape(level_count, row_count // WLAT, WLAT, col_count // WLON, WLON, last_dim)
    shaped = shaped.transpose(1, 3, 0, 2, 4, 5)
    return shaped.reshape(row_count // WLAT * (col_count // WLON), level_count * WLAT * WLON, last_dim)

def from_windows(field, level_count, row_count, col_count):
    last_dim = field.shape[-1]
    shaped = field.reshape(row_count // WLAT, col_count // WLON, level_count, WLAT, WLON, last_dim)
    shaped = shaped.transpose(2, 0, 3, 1, 4, 5)
    return shaped.reshape(level_count, row_count, col_count, last_dim)

def encode(levels, latent_queries, enc_kv, enc_out, enc_temp):
    level_total, row_count, col_count, features = levels.shape
    latent_count = latent_queries.shape[0]
    head_count = enc_temp.shape[0]
    head_size = features // head_count
    patch_count = row_count * col_count
    key_value = jnp.dot(levels.reshape(level_total * patch_count, features), enc_kv, preferred_element_type=jnp.float32).astype(jnp.bfloat16)
    key_value = key_value.reshape(level_total, patch_count, 2, head_count, head_size).astype(jnp.float32)
    key_value = jnp.transpose(key_value, (1, 0, 2, 3, 4))
    queries = latent_queries.astype(jnp.float32).reshape(1, latent_count, head_count, head_size)
    queries = jnp.broadcast_to(queries, (patch_count, latent_count, head_count, head_size))
    logit_scale = enc_temp / math.sqrt(head_size)
    context, probability, narrowed = attend(queries, key_value[:, :, 0], key_value[:, :, 1], None, logit_scale)
    context16 = jnp.transpose(context, (1, 0, 2, 3)).reshape(latent_count * patch_count, features).astype(jnp.bfloat16)
    mixed = jnp.dot(context16, enc_out, preferred_element_type=jnp.float32).reshape(latent_count, patch_count, features)
    encoded = (latent_queries.astype(jnp.float32)[:, None, :] + mixed).astype(jnp.bfloat16)
    encoded = encoded.reshape(latent_count, row_count, col_count, features)
    return (encoded, (queries, key_value, probability, narrowed, logit_scale))

def encode_back(saved, encoded_grad, enc_kv, enc_out):
    queries, key_value, probability, narrowed, logit_scale = saved
    patch_count, level_total = (key_value.shape[0], key_value.shape[1])
    latent_count, head_count, head_size = (queries.shape[1], queries.shape[2], queries.shape[3])
    features = head_count * head_size
    incoming = encoded_grad.reshape(latent_count * patch_count, features)
    context_grad = narrow(jnp.dot(incoming, enc_out.T, preferred_element_type=jnp.float32))
    context_grad = jnp.transpose(context_grad.reshape(latent_count, patch_count, head_count, head_size), (1, 0, 2, 3))
    unused, key_grad, value_grad = attend_back(queries, key_value[:, :, 0], key_value[:, :, 1], probability, narrowed, context_grad, logit_scale)
    kv_grad = jnp.stack([key_grad, value_grad], 2)
    kv_grad = jnp.transpose(kv_grad, (1, 0, 2, 3, 4)).reshape(level_total * patch_count, 2 * features).astype(jnp.bfloat16)
    return jnp.dot(kv_grad, enc_kv.T, preferred_element_type=jnp.float32).astype(jnp.bfloat16)

def swin_forward(rolled, wrap_flag, key_mask, w_qkv, w_out, swin_temp):
    level_count, row_count, col_count, features = rolled.shape
    head_count = swin_temp.shape[0]
    head_size = features // head_count
    unit, inverse = layer_norm(rolled.astype(jnp.float32))
    normed = to_windows(unit.astype(jnp.bfloat16))
    win_count, tok_count = (normed.shape[0], normed.shape[1])
    flattened = normed.reshape(win_count * tok_count, features)
    projected = jnp.dot(flattened, w_qkv, preferred_element_type=jnp.float32).astype(jnp.bfloat16)
    projected = projected.reshape(win_count, tok_count, 3, head_count, head_size).astype(jnp.float32)
    flag_grid = jnp.broadcast_to(wrap_flag[None, :, None, None], (level_count, row_count, col_count, 1))
    mask_grid = jnp.broadcast_to(key_mask[None, :, :, None], (level_count, row_count, col_count, 1))
    flag_win = to_windows(flag_grid)[:, :, 0]
    mask_win = to_windows(mask_grid)[:, :, 0]
    same_class = flag_win[:, :, None] == flag_win[:, None, :]
    diagonal = jnp.eye(tok_count, dtype=bool)[None]
    allowed = same_class & ((mask_win[:, None, :] == 1) | diagonal)
    logit_scale = swin_temp / math.sqrt(head_size)
    context, probability, narrowed = attend(projected[:, :, 0], projected[:, :, 1], projected[:, :, 2], allowed, logit_scale)
    context16 = context.reshape(win_count * tok_count, features).astype(jnp.bfloat16)
    attended = jnp.dot(context16, w_out, preferred_element_type=jnp.float32).astype(jnp.bfloat16)
    attended = from_windows(attended.reshape(win_count, tok_count, features), level_count, row_count, col_count)
    return (attended, (unit, inverse, flattened, projected, probability, narrowed, context16, logit_scale))

def swin_backward(saved, rolled_grad, w_qkv, w_out):
    unit, inverse, flattened, projected, probability, narrowed, context16, logit_scale = saved
    level_count, row_count, col_count, features = unit.shape
    win_count, tok_count = (projected.shape[0], projected.shape[1])
    head_count, head_size = (projected.shape[3], projected.shape[4])
    incoming = to_windows(rolled_grad).reshape(win_count * tok_count, features)
    term_out = lax.dot_general(context16, incoming, (((0,), (0,)), ((), ())), preferred_element_type=jnp.float32)
    context_grad = narrow(jnp.dot(incoming, w_out.T, preferred_element_type=jnp.float32))
    context_grad = context_grad.reshape(win_count, tok_count, head_count, head_size)
    query_grad, key_grad, value_grad = attend_back(projected[:, :, 0], projected[:, :, 1], projected[:, :, 2], probability, narrowed, context_grad, logit_scale)
    qkv_grad = jnp.stack([query_grad, key_grad, value_grad], 2).reshape(win_count * tok_count, 3 * features).astype(jnp.bfloat16)
    term_qkv = lax.dot_general(flattened, qkv_grad, (((0,), (0,)), ((), ())), preferred_element_type=jnp.float32)
    unit_grad = jnp.dot(qkv_grad, w_qkv.T, preferred_element_type=jnp.float32)
    unit_grad = from_windows(unit_grad.reshape(win_count, tok_count, features), level_count, row_count, col_count)
    rolled_x_grad = norm_back(unit, inverse, unit_grad).astype(jnp.bfloat16)
    return (rolled_x_grad, term_qkv, term_out)

def reference(levels_in, latent_queries, enc_kv, enc_out, enc_temp, w_qkv, w_out, swin_temp, lat_shift, lon_shift, key_valid, output_grad):
    lat_total = levels_in.shape[1]
    lon_total = levels_in.shape[2]
    block_count = lat_total // LAT_DEV
    lat_offset = lat_shift[0]
    lon_offset = lon_shift[0]

    def to_blocks(field):
        shaped = field.reshape(field.shape[0], block_count, LAT_DEV, lon_total, field.shape[3])
        return jnp.moveaxis(shaped, 1, 0)

    def from_blocks(field):
        shaped = jnp.moveaxis(field, 0, 1)
        return shaped.reshape(shaped.shape[0], lat_total, lon_total, shaped.shape[4])

    def encode_block(piece):
        return encode(piece, latent_queries, enc_kv, enc_out, enc_temp)[0]
    encoded = from_blocks(lax.map(encode_block, to_blocks(levels_in)))
    rolled = jnp.roll(encoded, (-lat_offset, -lon_offset), axis=(1, 2))
    rolled_grad = jnp.roll(output_grad, (-lat_offset, -lon_offset), axis=(1, 2))
    row_index = jnp.arange(lat_total, dtype=jnp.int32)
    wrap_flag = (row_index >= lat_total - lat_offset).astype(jnp.int32)

    def swin_block(pieces):
        piece, flag_piece, mask_piece, grad_piece = pieces
        attended, saved = swin_forward(piece, flag_piece, mask_piece, w_qkv, w_out, swin_temp)
        x_grad, term_qkv, term_out = swin_backward(saved, grad_piece, w_qkv, w_out)
        return (attended, x_grad, term_qkv, term_out)
    attended, x_grad, terms_qkv, terms_out = lax.map(swin_block, (to_blocks(rolled), wrap_flag.reshape(block_count, LAT_DEV), key_valid.reshape(block_count, LAT_DEV, lon_total), to_blocks(rolled_grad)))
    returned = jnp.roll(from_blocks(attended), (lat_offset, lon_offset), axis=(1, 2))
    output = (encoded.astype(jnp.float32) + returned.astype(jnp.float32)).astype(jnp.bfloat16)
    returned_grad = jnp.roll(from_blocks(x_grad), (lat_offset, lon_offset), axis=(1, 2))
    encoded_grad = (output_grad.astype(jnp.float32) + returned_grad.astype(jnp.float32)).astype(jnp.bfloat16)

    def back_block(pieces):
        piece, grad_piece = pieces
        saved = encode(piece, latent_queries, enc_kv, enc_out, enc_temp)[1]
        return encode_back(saved, grad_piece, enc_kv, enc_out).reshape(piece.shape)
    levels_grad = from_blocks(lax.map(back_block, (to_blocks(levels_in), to_blocks(encoded_grad))))
    factor = GRAD_GAIN * (encoded.shape[0] * lat_total * lon_total) ** (-0.5)
    w_qkv_grad = (lax.optimization_barrier(jnp.sum(terms_qkv, 0)) * factor).reshape(-1)
    w_out_grad = (lax.optimization_barrier(jnp.sum(terms_out, 0)) * factor).reshape(-1)
    return (output, levels_grad, w_qkv_grad, w_out_grad)
```

```python
import math

import jax
import jax.numpy as jnp
from jax import lax
from jax.experimental import pallas as pl
from jax.experimental.pallas import tpu as pltpu
from jax.sharding import PartitionSpec as P

MESH = pl.DeviceIdType.MESH
BF = jnp.bfloat16
F32 = jnp.float32

D = 512
HEADS = 16
HD = 32
LEVELS = 13
WLAT = 6
WLON = 12
PADC = 16
PATCH = WLAT * PADC
TOK = 2 * WLAT * WLON
HALF = WLAT * WLON
EDGE = 128
GRP = 8
GW = GRP * HD
GT = GRP * TOK
EPS = 1e-05
NEG = -1e30
GRAD_GAIN = 6.0
SCALE = 1.0 / math.sqrt(HD)

NY, NX, NZ = 4, 4, 8
WIDE = 1024
QW = 768
OW = 256

(
    C_GE, C_GN, C_EE, C_EN, C_AW, C_AS, C_XW, C_XS,
    C_TN, C_TR, C_TC, C_TQ,
) = range(12)
C_O1A = 12
C_O1B = 15
C_Q1A = 18
C_Q1B = 21
C_2A = 24
C_2B = 27
C_3A = 30
C_3B = 37
N_COPY = 44


def nt(a, b):
    return lax.dot_general(a, b, (((1,), (1,)), ((), ())), preferred_element_type=F32)


def nn(a, b):
    return lax.dot_general(a, b, (((1,), (0,)), ((), ())), preferred_element_type=F32)


def iota(shape, dim):
    return lax.broadcasted_iota(jnp.int32, shape, dim)


def split_token(t):
    level = (t >= HALF).astype(jnp.int32)
    rest = t - HALF * level
    row = lax.shift_right_logical(rest * 171, 11)
    return level, row, rest - row * WLON


def split_edge(u):
    level = (u >= 60).astype(jnp.int32)
    rest = u - 60 * level
    row = lax.shift_right_logical(rest * 171, 11)
    return level, row, rest - row * WLON


def one_hot(index, keep, width):
    shape = (index.shape[0], width)
    return jnp.where(keep & (index == iota(shape, 1)), 1.0, 0.0).astype(BF)


def padded(block):
    lead = block.shape[0]
    full = jnp.concatenate([block, jnp.zeros((lead, PADC - WLON, D), block.dtype)], 1)
    return full.reshape(lead * PADC, D)


def lanes_of(values, shape, dim, step):
    index = iota(shape, dim)
    out = jnp.zeros(shape, F32)
    for k, v in enumerate(values):
        out = jnp.where((index >= k * step) & (index < (k + 1) * step), v, out)
    return out


def kernel(
    lev_hbm, q_ref, kvw_hbm, eo_hbm, etemp_ref, wq_hbm, wo_hbm, stemp_ref, lats_ref, lons_ref, valid_ref, og_ref,
    out_ref, lg_ref, gq_ref, go_ref,
    lev, kvw, eo, wq, wo,
    levp, vals, prob, wexp, prod, vgrad, encp, score,
    own_e, re_e, sn_e, rn_e, own_g, re_g, sn_g, rn_g,
    att, rw_a, ss_a, rs_a, xg, rw_x, ss_x, rs_x,
    unit, qkv, normed, rgrad, ctx, qgrad,
    m_normed, m_rgrad, m_ctx, m_qgrad,
    qs, cgs, pt, p16, bias, hmask, fold,
    send_a, send_b, r1a, r1b, s2a, s2b, r2a, r2b, s3a, s3b, r3a, r3b,
    lsem, ssem, rsem,
):
    lat = lax.axis_index("lat")
    lon = lax.axis_index("lon")
    y_hi = lat // 8
    x = (lat // 2) % 4
    core = lat % 2
    z = lon // 2
    y_lo = lon % 2
    y = y_hi * 2 + y_lo

    def device(yy, xx, cc, zz):
        return ((yy // 2) * 8 + xx * 2 + cc, zz * 2 + yy % 2)

    mate = (lat + 1 - 2 * core, lon)
    east = (lat, (lon + 1) % 16)
    west = (lat, (lon + 15) % 16)
    north = ((lat + 1) % 16, lon)
    south = ((lat + 15) % 16, lon)
    y_peers = [device((y + k) % NY, x, core, z) for k in range(1, NY)]
    x_peers = [device(y, (x + k) % NX, core, z) for k in range(1, NX)]
    z_peers = [device(y, x, core, (z + k) % NZ) for k in range(1, NZ)]
    greeted = [mate, east, west, north, south] + y_peers + x_peers + z_peers
    barrier = pltpu.get_barrier_semaphore()
    for peer in greeted:
        pl.semaphore_signal(barrier, inc=1, device_id=peer, device_id_type=MESH)

    loads = [
        pltpu.make_async_copy(src, dst, lsem.at[i])
        for i, (src, dst) in enumerate(
            [(kvw_hbm, kvw), (lev_hbm, lev), (eo_hbm, eo), (wq_hbm, wq), (wo_hbm, wo)]
        )
    ]
    for load in loads:
        load.start()

    started = []

    def send(src, dst, index, peer):
        copy = pltpu.make_async_remote_copy(
            src_ref=src, dst_ref=dst, send_sem=ssem.at[index], recv_sem=rsem.at[index],
            device_id=peer, device_id_type=MESH,
        )
        copy.start()
        started.append(copy)
        return copy

    s = lats_ref[0]
    t = lons_ref[0]

    tok = iota((TOK, 1), 0)
    lv, ri, cj = split_token(tok)
    i2 = ri + s
    j2 = cj + t
    in_n = i2 >= WLAT
    in_e = j2 >= WLON
    base = lv * HALF + i2 * WLON + j2
    sel_own = one_hot(base, (~in_n) & (~in_e), TOK)
    sel_e = one_hot(base - WLON, (~in_n) & in_e, TOK)
    sel_n = one_hot(lv * 60 + (i2 - WLAT) * WLON + cj, in_n, EDGE)
    edge = iota((EDGE, 1), 0)
    elv, er, ec = split_edge(edge)
    real = edge < 120
    ej = ec + t
    ebase = elv * HALF + er * WLON + ej
    edge_own = one_hot(ebase, real & (ej < WLON), TOK)
    edge_e = one_hot(ebase - WLON, real & (ej >= WLON), TOK)
    compact = one_hot((lv * WLAT + ri) * PADC + cj, tok >= 0, 2 * PATCH)

    own_g[...] = nn(compact, jnp.concatenate([padded(og_ref[0]), padded(og_ref[1])], 0)).astype(BF)
    pl.semaphore_wait(barrier, len(greeted))
    ge = send(own_g, re_g, C_GE, west)

    q_rows = jnp.concatenate([jnp.broadcast_to(q_ref[l : l + 1, :], (HEADS, D)) for l in range(2)], 0)
    row_head = iota((2 * HEADS, D), 0) % HEADS
    lane_head = lax.shift_right_logical(iota((2 * HEADS, D), 1), 5)
    q_rows = jnp.where(row_head == lane_head, q_rows.astype(F32), 0.0).astype(BF)
    enc_scale = [etemp_ref[h] * SCALE for h in range(HEADS)]
    loads[0].wait()
    key_q = nt(q_rows, kvw[:, :D])
    folded = key_q * lanes_of(enc_scale * 2, (2 * HEADS, 1), 0, 1)
    fold_hi = folded.astype(BF)
    fold_lo = (folded - fold_hi.astype(F32)).astype(BF)
    loads[1].wait()
    for m in range(LEVELS):
        levp[m * PATCH : (m + 1) * PATCH, :] = padded(lev[m])
    for m in range(LEVELS):
        rows = slice(m * PATCH, (m + 1) * PATCH)
        level = levp[rows, :]
        vals[rows, :] = nn(level, kvw[:, D:]).astype(BF)
        score[m] = nt(level, fold_hi) + nt(level, fold_lo)
    peak = score[0]
    for m in range(1, LEVELS):
        peak = jnp.maximum(peak, score[m])
    total = jnp.zeros_like(peak)
    for m in range(LEVELS):
        e = jnp.exp(score[m] - peak)
        score[m] = e
        total = total + e
    inverse = 1.0 / total
    spread_row = iota((2 * HEADS, 2 * D), 0)
    spread = jnp.where(lax.shift_right_logical(iota((2 * HEADS, 2 * D), 1), 5) == spread_row, 1.0, 0.0).astype(BF)
    for m in range(LEVELS):
        pm = score[m] * inverse
        prob[m] = pm
        wexp[m * PATCH : (m + 1) * PATCH, :] = nn(pm.astype(BF), spread).astype(BF)
    for r in range(WLAT):
        acc0 = jnp.zeros((PADC, D), F32)
        acc1 = jnp.zeros((PADC, D), F32)
        for m in range(LEVELS):
            rows = slice(m * PATCH + r * PADC, m * PATCH + (r + 1) * PADC)
            v = vals[rows, :].astype(F32)
            acc0 = acc0 + wexp[rows, :D].astype(F32) * v
            acc1 = acc1 + wexp[rows, D:].astype(F32) * v
        encp[r * PADC : (r + 1) * PADC, :] = acc0.astype(BF)
        encp[PATCH + r * PADC : PATCH + (r + 1) * PADC, :] = acc1.astype(BF)
    loads[2].wait()
    mixed = nn(encp[...], eo[...])
    encoded = jnp.concatenate(
        [q_ref[l : l + 1, :].astype(F32) + mixed[l * PATCH : (l + 1) * PATCH, :] for l in range(2)], 0
    ).astype(BF)
    encp[...] = encoded
    own_e[...] = nn(compact, encoded).astype(BF)
    ee = send(own_e, re_e, C_EE, west)

    ge.wait_recv()
    sn_g[...] = (nn(edge_own, own_g[...]) + nn(edge_e, re_g[...])).astype(BF)
    gn = send(sn_g, rn_g, C_GN, south)
    tq = iota((1, GT), 1)
    for k in range(1, GRP):
        tq = jnp.where(iota((1, GT), 1) >= k * TOK, iota((1, GT), 1) - k * TOK, tq)
    qlv, qri, qcj = split_token(tq)
    first_wrapped = 96 - s
    wrap_k = (lat * WLAT + ri) >= first_wrapped
    wrap_q = (lat * WLAT + qri) >= first_wrapped
    lane = iota((TOK, WLON), 1)
    valid_row = jnp.zeros((TOK, WLON), jnp.int32)
    for r in range(WLAT):
        valid_row = jnp.where(ri == r, valid_ref[r : r + 1, :], valid_row)
    valid_k = jnp.sum(jnp.where(lane == cj, valid_row, 0), 1, keepdims=True)
    kk = iota((TOK, GT), 0)
    wk = jnp.where(wrap_k, 1, 0)
    wqv = jnp.where(wrap_q, 1, 0)
    ok = (wk == wqv) & ((valid_k == 1) | (kk == tq))
    bias[...] = jnp.where(ok, 0.0, NEG)
    fold[...] = jnp.where(kk == tq, 1.0, 0.0).astype(BF)
    fh = lax.shift_right_logical(iota((GW, GT), 0), 5)
    lane_t = iota((GW, GT), 1)
    hmask[...] = jnp.where((lane_t >= fh * TOK) & (lane_t < (fh + 1) * TOK), 1.0, 0.0).astype(BF)
    group_head = lax.shift_right_logical(iota((TOK, GW), 1), 5)
    eye = jnp.where(iota((GW, GW), 0) == iota((GW, GW), 1), 1.0, 0.0).astype(BF)
    scale_rows = [
        lanes_of([stemp_ref[g * GRP + h] * SCALE for h in range(GRP)], (1, GT), 1, TOK) for g in range(2)
    ]
    n = iota((256, 1), 0)
    bit = lambda shift, mask: lax.shift_right_logical(n, shift) & mask
    wrow = bit(7, 1) * 256 + bit(4, 3) * 64 + core * 32 + bit(1, 7) * 4 + bit(6, 1) * 2 + (n & 1)
    pick = one_hot(wrow, n >= 0, D)

    gn.wait_recv()
    rgrad[...] = (nn(sel_own, own_g[...]) + nn(sel_e, re_g[...]) + nn(sel_n, rn_g[...])).astype(BF)
    tr = send(rgrad, m_rgrad, C_TR, mate)
    loads[4].wait()
    cgrad = nt(rgrad[...], wo[...]).astype(BF)
    for g in range(2):
        part = cgrad[:, g * GW : (g + 1) * GW]
        for h in range(GRP):
            cgs[g, h * TOK : (h + 1) * TOK, :] = jnp.where(group_head == h, part, jnp.zeros_like(part))

    ee.wait_recv()
    sn_e[...] = (nn(edge_own, own_e[...]) + nn(edge_e, re_e[...])).astype(BF)
    en = send(sn_e, rn_e, C_EN, south)
    near = nn(sel_own, own_e[...]) + nn(sel_e, re_e[...])
    en.wait_recv()
    rolled = near + nn(sel_n, rn_e[...])

    mean = jnp.mean(rolled, 1, keepdims=True)
    centered = rolled - mean
    inv = lax.rsqrt(jnp.mean(centered * centered, 1, keepdims=True) + EPS)
    unit_v = centered * inv
    unit[...] = unit_v
    normed[...] = unit_v.astype(BF)
    tn = send(normed, m_normed, C_TN, mate)
    loads[3].wait()
    qkv[...] = nn(normed[...], wq[...]).astype(BF)
    for g in range(2):
        lanes = slice(g * GW, (g + 1) * GW)
        qg = qkv[:, g * GW : (g + 1) * GW]
        for h in range(GRP):
            qs[g, h * TOK : (h + 1) * TOK, :] = jnp.where(group_head == h, qg, jnp.zeros_like(qg))
        st = nt(qkv[:, D + g * GW : D + (g + 1) * GW], qs[g]) * scale_rows[g] + bias[...]
        e = jnp.exp(st - jnp.max(st, 0, keepdims=True))
        p = e * (1.0 / jnp.sum(e, 0, keepdims=True))
        pt[g] = p
        p16[g] = p.astype(BF)
        v_t = nt(eye, qkv[:, 2 * D + g * GW : 2 * D + (g + 1) * GW]).astype(BF)
        c_t = nn(v_t, p16[g]).astype(BF) * hmask[...]
        ctx[:, lanes] = nt(fold[...], c_t).astype(BF)
    tc = send(ctx, m_ctx, C_TC, mate)
    att[...] = nn(ctx[...], wo[...]).astype(BF)
    aw = send(att, rw_a, C_AW, east)

    for g in range(2):
        lanes = slice(g * GW, (g + 1) * GW)
        p = pt[g]
        dp = nt(qkv[:, 2 * D + g * GW : 2 * D + (g + 1) * GW], cgs[g])
        ds = p * (dp - jnp.sum(p * dp, 0, keepdims=True)) * scale_rows[g]
        ds16 = ds.astype(BF)
        kg = qkv[:, D + g * GW : D + (g + 1) * GW]
        k_t = nt(eye, kg).astype(BF)
        q_t = nn(k_t, ds16).astype(BF) * hmask[...]
        qgrad[:, lanes] = nt(fold[...], q_t).astype(BF)
        qgrad[:, D + g * GW : D + (g + 1) * GW] = nn(ds16, qs[g]).astype(BF)
        qgrad[:, 2 * D + g * GW : 2 * D + (g + 1) * GW] = nn(p16[g], cgs[g]).astype(BF)
    tqc = send(qgrad, m_qgrad, C_TQ, mate)

    ugrad = nt(qgrad[...], wq[...])
    u = unit[...]
    xgrad = inv * (
        ugrad - jnp.mean(ugrad, 1, keepdims=True) - u * jnp.mean(ugrad * u, 1, keepdims=True)
    )
    xg[...] = xgrad.astype(BF)
    xw = send(xg, rw_x, C_XW, east)

    bl, br, bc = elv, er + 1, ec
    back_j = bc - t
    bbase = bl * HALF + br * WLON + back_j
    bedge_own = one_hot(bbase, real & (back_j >= 0), TOK)
    bedge_w = one_hot(bbase + WLON, real & (back_j < 0), TOK)
    pp = iota((2 * PATCH, 1), 0)
    pl_ = (pp >= PATCH).astype(jnp.int32)
    prest = pp - PATCH * pl_
    pr = lax.shift_right_logical(prest, 4)
    pc = prest & 15
    inside = pc < WLON
    ii = pr - s
    jj = pc - t
    pbase = pl_ * HALF + ii * WLON + jj
    pad_own = one_hot(pbase, inside & (ii >= 0) & (jj >= 0), TOK)
    pad_w = one_hot(pbase + WLON, inside & (ii >= 0) & (jj < 0), TOK)
    pad_s = one_hot(pl_ * 60 + (ii + WLAT - 1) * WLON + pc, inside & (ii < 0), EDGE)

    aw.wait_recv()
    ss_a[...] = (nn(bedge_own, att[...]) + nn(bedge_w, rw_a[...])).astype(BF)
    as_ = send(ss_a, rs_a, C_AS, north)

    def chip_sum(left, m_left, right, m_right):
        mine = nt(pick, left[...]).astype(BF)
        other = nt(pick, m_left[...]).astype(BF)
        return nn(mine, right[...]) + nn(other, m_right[...])

    def share(width, low, slab_a, slab_b, first_a, first_b):
        for k in range(1, NY):
            src = send_a.at[(y + k) % NY, :, :, pl.ds(low, width)]
            slab_a.append(send(src, r1a.at[k - 1, :, :, pl.ds(low, width)], first_a + k - 1, y_peers[k - 1]))
        for k in range(1, NX):
            src = send_b.at[:, (x + k) % NX, :, pl.ds(low, width)]
            slab_b.append(send(src, r1b.at[k - 1, :, :, pl.ds(low, width)], first_b + k - 1, x_peers[k - 1]))

    first_stage = []
    tc.wait_recv()
    tr.wait_recv()
    g_out = chip_sum(ctx, m_ctx, rgrad, m_rgrad).astype(BF).reshape(NY, NX, 16, D)
    send_a[:, :, :, QW:] = g_out[:, :, :, :OW]
    send_b[:, :, :, QW:] = g_out[:, :, :, OW:]
    share(OW, QW, first_stage, first_stage, C_O1A, C_O1B)
    tn.wait_recv()
    tqc.wait_recv()
    g_qkv = chip_sum(normed, m_normed, qgrad, m_qgrad).astype(BF).reshape(NY, NX, 16, 3 * D)
    send_a[:, :, :, :QW] = g_qkv[:, :, :, :QW]
    send_b[:, :, :, :QW] = g_qkv[:, :, :, QW:]
    share(QW, 0, first_stage, first_stage, C_Q1A, C_Q1B)

    xw.wait_recv()
    ss_x[...] = (nn(bedge_own, xg[...]) + nn(bedge_w, rw_x[...])).astype(BF)
    xs = send(ss_x, rs_x, C_XS, north)
    as_.wait_recv()
    back_a = nn(pad_own, att[...]) + nn(pad_w, rw_a[...]) + nn(pad_s, rs_a[...])
    out16 = (encp[...].astype(F32) + back_a).astype(BF)
    out_ref[...] = out16.reshape(2, WLAT, PADC, D)[:, :, :WLON, :]
    xs.wait_recv()
    back_x = nn(pad_own, xg[...]) + nn(pad_w, rw_x[...]) + nn(pad_s, rs_x[...])
    og_pad = jnp.concatenate([padded(og_ref[0]), padded(og_ref[1])], 0)
    egrad = (og_pad.astype(F32) + back_x).astype(BF)

    encp[...] = nt(egrad, eo[...]).astype(BF)

    def products(r):
        c0 = encp[r * PADC : (r + 1) * PADC, :].astype(F32)
        c1 = encp[PATCH + r * PADC : PATCH + (r + 1) * PADC, :].astype(F32)
        for m in range(LEVELS):
            rows = slice(m * PATCH + r * PADC, m * PATCH + (r + 1) * PADC)
            v = vals[rows, :].astype(F32)
            prod[rows, :D] = (c0 * v).astype(BF)
            prod[rows, D:] = (c1 * v).astype(BF)
            vgrad[rows, :] = (wexp[rows, :D].astype(F32) * c0 + wexp[rows, D:].astype(F32) * c1).astype(BF)

    for r in range(WLAT):
        products(r)

    for copy in first_stage:
        copy.wait_recv()
    sum_a = send_a[y].astype(F32)
    sum_b = send_b[:, x].astype(F32)
    for k in range(3):
        sum_a = sum_a + r1a[k].astype(F32)
        sum_b = sum_b + r1b[k].astype(F32)
    s2a[...] = sum_a.astype(BF)
    s2b[...] = sum_b.astype(BF)
    second_stage = []
    for k in range(1, NX):
        second_stage.append(send(s2a.at[(x + k) % NX], r2a.at[k - 1], C_2A + k - 1, x_peers[k - 1]))
    for k in range(1, NY):
        second_stage.append(send(s2b.at[(y + k) % NY], r2b.at[k - 1], C_2B + k - 1, y_peers[k - 1]))

    sums = jnp.zeros((PATCH, 2 * HEADS), F32)
    for m in range(LEVELS):
        pg = nt(prod[m * PATCH : (m + 1) * PATCH, :], spread)
        score[m] = pg
        sums = sums + prob[m] * pg
    lane_scale = lanes_of(enc_scale * 2, (1, 2 * HEADS), 1, 1)

    for copy in second_stage:
        copy.wait_recv()
    last_a = s2a[x].astype(F32)
    last_b = s2b[y].astype(F32)
    for k in range(3):
        last_a = last_a + r2a[k].astype(F32)
        last_b = last_b + r2b[k].astype(F32)
    for k in range(NZ):
        s3a[k] = last_a[2 * k : 2 * k + 2, :]
        s3b[k] = last_b[2 * k : 2 * k + 2, :]
    third_stage = []
    for k in range(1, NZ):
        third_stage.append(send(s3a.at[(z + k) % NZ], r3a.at[k - 1], C_3A + k - 1, z_peers[k - 1]))
        third_stage.append(send(s3b.at[(z + k) % NZ], r3b.at[k - 1], C_3B + k - 1, z_peers[k - 1]))

    key_q16 = key_q.astype(BF)
    for m in range(LEVELS):
        rows = slice(m * PATCH, (m + 1) * PATCH)
        sg = prob[m] * (score[m] - sums) * lane_scale
        lg = nt(vgrad[rows, :], kvw[:, D:]) + nn(sg.astype(BF), key_q16)
        lg_ref[m] = lg.astype(BF).reshape(WLAT, PADC, D)[:, :WLON, :]

    for copy in third_stage:
        copy.wait_recv()
    fin_a = s3a[z]
    fin_b = s3b[z]
    for k in range(NZ - 1):
        fin_a = fin_a + r3a[k]
        fin_b = fin_b + r3b[k]
    factor = GRAD_GAIN * (2 * 96 * 192) ** (-0.5)
    gq_ref[:, :QW] = fin_a[:, :QW] * factor
    gq_ref[:, QW:] = fin_b[:, :QW] * factor
    go_ref[:, :OW] = fin_a[:, QW:] * factor
    go_ref[:, OW:] = fin_b[:, QW:] * factor
    for copy in started:
        copy.wait_send()


def local(levels_in, latent_queries, enc_kv, enc_out, enc_temp, w_qkv, w_out, swin_temp, lat_shift, lon_shift, key_valid, output_grad):
    vmem = pl.BlockSpec(memory_space=pltpu.VMEM)
    smem = pl.BlockSpec(memory_space=pltpu.SMEM)
    hbm = pl.BlockSpec(memory_space=pl.ANY)
    V = pltpu.VMEM
    block = lambda rows: V((rows, D), BF)
    scratch = [
        V((LEVELS, WLAT, WLON, D), BF), V((D, 2 * D), BF), V((D, D), BF), V((D, 3 * D), BF), V((D, D), BF),
        V((LEVELS * PATCH, D), BF),
        V((LEVELS * PATCH, D), BF),
        V((LEVELS, PATCH, 2 * HEADS), F32),
        V((LEVELS * PATCH, 2 * D), BF),
        V((LEVELS * PATCH, 2 * D), BF),
        V((LEVELS * PATCH, D), BF),
        block(2 * PATCH),
        V((LEVELS, PATCH, 2 * HEADS), F32),
        block(TOK), block(TOK), block(EDGE), block(EDGE),
        block(TOK), block(TOK), block(EDGE), block(EDGE),
        block(TOK), block(TOK), block(EDGE), block(EDGE),
        block(TOK), block(TOK), block(EDGE), block(EDGE),
        V((TOK, D), F32), V((TOK, 3 * D), BF), block(TOK), block(TOK), block(TOK), V((TOK, 3 * D), BF),
        block(TOK), block(TOK), block(TOK), V((TOK, 3 * D), BF),
        V((2, GT, GW), BF), V((2, GT, GW), BF), V((2, TOK, GT), F32), V((2, TOK, GT), BF),
        V((TOK, GT), F32), V((GW, GT), BF), V((TOK, GT), BF),
        V((NY, NX, 16, WIDE), BF), V((NY, NX, 16, WIDE), BF),
        V((3, NX, 16, WIDE), BF), V((3, NY, 16, WIDE), BF),
        V((NX, 16, WIDE), BF), V((NY, 16, WIDE), BF),
        V((3, 16, WIDE), BF), V((3, 16, WIDE), BF),
        V((NZ, 2, WIDE), F32), V((NZ, 2, WIDE), F32),
        V((NZ - 1, 2, WIDE), F32), V((NZ - 1, 2, WIDE), F32),
        pltpu.SemaphoreType.DMA((5,)),
        pltpu.SemaphoreType.DMA((N_COPY,)),
        pltpu.SemaphoreType.DMA((N_COPY,)),
    ]
    out, lg, gq, go = pl.pallas_call(
        kernel,
        out_shape=(
            jax.ShapeDtypeStruct((2, WLAT, WLON, D), BF),
            jax.ShapeDtypeStruct((LEVELS, WLAT, WLON, D), BF),
            jax.ShapeDtypeStruct((2, 3 * D), F32),
            jax.ShapeDtypeStruct((2, D), F32),
        ),
        in_specs=[hbm, vmem, hbm, hbm, smem, hbm, hbm, smem, smem, smem, vmem, vmem],
        out_specs=(vmem, vmem, vmem, vmem),
        scratch_shapes=scratch,
        compiler_params=pltpu.CompilerParams(
            collective_id=0, has_side_effects=True, vmem_limit_bytes=56 * 1024 * 1024
        ),
    )(levels_in, latent_queries, enc_kv, enc_out, enc_temp, w_qkv, w_out, swin_temp, lat_shift, lon_shift, key_valid, output_grad)
    return out, lg, gq.reshape(-1), go.reshape(-1)


def solution(mesh):
    return jax.shard_map(
        local,
        mesh=mesh,
        in_specs=(
            P(None, "lat", "lon", None), P(), P(), P(), P(), P(), P(), P(), P(), P(),
            P("lat", "lon"),
            P(None, "lat", "lon", None),
        ),
        out_specs=(
            P(None, "lat", "lon", None),
            P(None, "lat", "lon", None),
            P(("lat", "lon")),
            P(("lat", "lon")),
        ),
        check_vma=False,
    )
```

```python
import functools
import math

import jax
import jax.numpy as jnp
from jax import lax
from jax.experimental import pallas as pl
from jax.experimental.pallas import tpu as pltpu
from jax.sharding import PartitionSpec as P

MESH = pl.DeviceIdType.MESH
BF = jnp.bfloat16
F32 = jnp.float32

D = 512
HEADS = 16
HD = 32
LEVELS = 13
WLAT = 6
WLON = 12
PADL = 16
TOK = 2 * WLAT * WLON
HALF = WLAT * WLON
ROWS = HALF * PADL
CHUNK = 384
GRP = 8
GW = GRP * HD
GT = GRP * TOK
EPS = 1e-05
NEG = -1e30
GRAD_GAIN = 6.0
SCALE = 1.0 / math.sqrt(HD)

NY, NX, NZ = 4, 4, 8
WIDE = 1024
EARLY = 512
SIDE = 80
PAIR = 2 * SIDE

C_GE, C_EE, C_AW, C_XW, C_TN, C_TR, C_TC, C_TV, C_TQ0, C_TQ1 = range(10)
C_GN, C_EN, C_AS, C_XS = range(10, 18, 2)
C_E1A, C_E1B, C_M1A, C_M1B, C_L1A, C_L1B, C_2A, C_2B = range(18, 42, 3)
C_3 = 42
N_COPY = 49


def nt(a, b):
    return lax.dot_general(a, b, (((1,), (1,)), ((), ())), preferred_element_type=F32)


def nn(a, b):
    return lax.dot_general(a, b, (((1,), (0,)), ((), ())), preferred_element_type=F32)


def iota(shape, dim):
    return lax.broadcasted_iota(jnp.int32, shape, dim)


def split_token(t):
    level = (t >= HALF).astype(jnp.int32)
    rest = t - HALF * level
    row = lax.shift_right_logical(rest * 171, 11)
    return level, row, rest - row * WLON


def split_side(u, width):
    half = (u >= SIDE).astype(jnp.int32)
    rest = u - SIDE * half
    real = rest < HALF
    level = (rest >= HALF // 2).astype(jnp.int32)
    rest = rest - HALF // 2 * level
    row = lax.shift_right_logical(rest * 171, 11) if width == WLON else lax.shift_right_logical(rest * 43, 8)
    return half, level, row, rest - row * width, real


def one_hot(index, keep, width):
    shape = (index.shape[0], width)
    return jnp.where(keep & (index == iota(shape, 1)), 1.0, 0.0).astype(BF)


def roll_matrices(row_step, col_step, from_east):
    lv, ri, cj = split_token(iota((TOK, 1), 0))
    half, elv, er, ec, real = split_side(iota((PAIR, 1), 0), WLON)

    def along_lon(level, row, col, keep):
        inside = (col >= 0) & (col < WLON)
        own = one_hot(level * HALF + row * WLON + col, keep & inside, TOK)
        start = level * (HALF // 2) + row * (WLON // 2)
        side = start + col + (-WLON if from_east else WLON // 2)
        return own, one_hot(side, keep & (~inside), SIDE)

    row = ri + row_step
    here = (row >= 0) & (row < WLAT)
    own, side = along_lon(lv, row, cj + col_step, here)
    start = lv * (HALF // 2) + cj
    over = jnp.where(row >= WLAT, start + (row - WLAT) * WLON, SIDE + start + (row + 3) * WLON)
    far = one_hot(over, ~here, PAIR)
    edge_own, edge_side = along_lon(elv, er + 3 * half, ec + col_step, real)
    return own, side, far, edge_own, edge_side


def lanes_of(values, shape, dim, step):
    index = iota(shape, dim)
    out = jnp.zeros(shape, F32)
    for k, v in enumerate(values):
        out = jnp.where((index >= k * step) & (index < (k + 1) * step), v, out)
    return out


def kernel(
    late_col,
    lev_hbm, q_ref, kvw_hbm, eo_hbm, etemp_ref, wq_hbm, wo_hbm, stemp_ref, lats_ref, lons_ref, valid_ref, og_hbm,
    out_ref, lg_ref, gq_ref, go_ref,
    lev, kvw, eo, wq, wo, og,
    levp, vals, prob, wexp, prod, vgrad, part, cback, rows_f, kvp, out_v, lg_v,
    own_e, pk_e, rl_e, sn_e, rn_e,
    own_g, pk_g, rl_g, sn_g, rn_g,
    att, pk_a, rl_a, sn_a, rn_a,
    xg, pk_x, rl_x, sn_x, rn_x,
    unit, qkv, normed, rgrad, ctx, vback, qback,
    m_normed, m_rgrad, m_ctx, m_vback, m_qback,
    qs, cgs, pt, p16, bias, hmask, fold,
    send_a, send_b, r1a, r1b, s2a, s2b, r2a, r2b, s3f, s3, r3,
    lsem, ssem, rsem,
):
    lat = lax.axis_index("lat")
    lon = lax.axis_index("lon")
    y_hi = lat // 8
    x = (lat // 2) % 4
    core = lat % 2
    z = lon // 2
    y_lo = lon % 2
    y = y_hi * 2 + y_lo

    def device(yy, xx, cc, zz):
        return ((yy // 2) * 8 + xx * 2 + cc, zz * 2 + yy % 2)

    mate = (lat + 1 - 2 * core, lon)
    east = (lat, (lon + 1) % 16)
    west = (lat, (lon + 15) % 16)
    north = ((lat + 1) % 16, lon)
    south = ((lat + 15) % 16, lon)
    y_peers = [device((y + k) % NY, x, core, z) for k in range(1, NY)]
    x_peers = [device(y, (x + k) % NX, core, z) for k in range(1, NX)]
    z_peers = [device(y, x, core, (z + k) % NZ) for k in range(1, NZ)]
    greeted = [mate, east, west, north, south] + y_peers + x_peers + z_peers
    barrier = pltpu.get_barrier_semaphore()
    for peer in greeted:
        pl.semaphore_signal(barrier, inc=1, device_id=peer, device_id_type=MESH)

    loads = [
        pltpu.make_async_copy(src, dst, lsem.at[i])
        for i, (src, dst) in enumerate(
            [(kvw_hbm, kvw), (lev_hbm, lev), (eo_hbm, eo), (wq_hbm, wq), (wo_hbm, wo), (og_hbm, og)]
        )
    ]
    for i in (5, 0, 1, 2, 3, 4):
        loads[i].start()

    started = []

    def send(src, dst, index, peer):
        copy = pltpu.make_async_remote_copy(
            src_ref=src, dst_ref=dst, send_sem=ssem.at[index], recv_sem=rsem.at[index],
            device_id=peer, device_id_type=MESH,
        )
        copy.start()
        started.append(copy)
        return copy

    def send_pair(src, dst, index, first, second):
        halves = [pl.ds(0, SIDE), pl.ds(SIDE, SIDE)]
        return [
            send(src.at[h], dst.at[h], index + i, peer) for i, (h, peer) in enumerate(zip(halves, (first, second)))
        ]

    def arrived(copies):
        for copy in copies:
            copy.wait_recv()

    s = lats_ref[0]
    t = lons_ref[0]
    late_row = s > WLAT // 2
    row_step = jnp.where(late_row, s - WLAT, s)
    col_step = t - WLON if late_col else t
    ahead, back = (east, west) if late_col else (west, east)

    q_rows = jnp.concatenate([jnp.broadcast_to(q_ref[l : l + 1, :], (HEADS, D)) for l in range(2)], 0)
    row_head = iota((2 * HEADS, D), 0) % HEADS
    lane_head = lax.shift_right_logical(iota((2 * HEADS, D), 1), 5)
    q_rows = jnp.where(row_head == lane_head, q_rows.astype(F32), 0.0).astype(BF)
    lane_scale = lanes_of([etemp_ref[h] * SCALE for h in range(HEADS)] * 2, (1, 2 * HEADS), 1, 1)
    loads[0].wait()
    loads[1].wait()
    filler = jnp.zeros((8, PADL - LEVELS, D), BF)
    for c in range(HALF // 8):
        block = jnp.concatenate([lev[8 * c : 8 * c + 8], filler], 1)
        levp[8 * PADL * c : 8 * PADL * (c + 1), :] = block.reshape(8 * PADL, D)
    real_level = iota((CHUNK // PADL, PADL, 2 * HEADS), 1) < LEVELS
    for c in range(ROWS // CHUNK):
        rows = slice(c * CHUNK, (c + 1) * CHUNK)
        kv = nn(levp[rows, :], kvw[...])
        vals[rows, :] = kv[:, D:].astype(BF)
        sc = (nt(kv[:, :D].astype(BF), q_rows) * lane_scale).reshape(CHUNK // PADL, PADL, 2 * HEADS)
        sc = jnp.where(real_level, sc, NEG)
        e = jnp.exp(sc - jnp.max(sc, 1, keepdims=True))
        pm = e * (1.0 / jnp.sum(e, 1, keepdims=True))
        prob[rows, :] = pm.reshape(CHUNK, 2 * HEADS)
    spread_row = iota((2 * HEADS, 2 * D), 0)
    spread = jnp.where(lax.shift_right_logical(iota((2 * HEADS, 2 * D), 1), 5) == spread_row, 1.0, 0.0).astype(BF)
    for c in range(HALF // 8):
        rows = slice(8 * PADL * c, 8 * PADL * (c + 1))
        w = nn(prob[rows, :].astype(BF), spread)
        wexp[rows, :] = w.astype(BF)
        v = vals[rows, :].astype(F32)
        for l in range(2):
            product = (w[:, l * D : (l + 1) * D] * v).reshape(8, 2, 8, D)
            product = (product[:, 0] + product[:, 1]).reshape(64, D)
            for j in range(4):
                part[4 * l + j, 64 * c : 64 * (c + 1), :] = product[:, 128 * j : 128 * (j + 1)]
        for l in range(2):
            for j in range(4):
                acc = part[4 * l + j, pl.ds(64 * c, 8, stride=8), :]
                for m in range(1, 8):
                    acc = acc + part[4 * l + j, pl.ds(64 * c + m, 8, stride=8), :]
                cback[l * HALF + 8 * c : l * HALF + 8 * (c + 1), 128 * j : 128 * (j + 1)] = acc
    loads[2].wait()
    mixed = nn(cback[...].astype(BF), eo[...])
    token_level = iota((TOK, D), 0) >= HALF
    query = jnp.where(token_level, q_ref[1:2, :].astype(F32), q_ref[0:1, :].astype(F32))
    enc16 = (query + mixed).astype(BF)
    own_e[...] = enc16
    _, plv, pr, pc, preal = split_side(iota((SIDE, 1), 0), WLON // 2)
    packs = [one_hot(plv * HALF + pr * WLON + pc + half * (WLON // 2), preal, TOK) for half in range(2)]
    pack_ahead, pack_back = packs[::-1] if late_col else packs
    kvp[...] = jnp.zeros((8, D), F32)
    kvp[0:WLAT, 0:WLON] = valid_ref[...].astype(F32)

    def with_valid(pair, valid_rows):
        return jnp.concatenate([pair[: pair.shape[0] - 8], valid_rows], 0).astype(BF)

    def valid_of(message):
        return message[message.shape[0] - 8 :, :].astype(F32)

    pk_e[...] = with_valid(nn(pack_ahead, enc16), kvp[...])
    pl.semaphore_wait(barrier, len(greeted))
    ee = send(pk_e, rl_e, C_EE, ahead)

    tok = iota((TOK, 1), 0)
    lv, ri, cj = split_token(tok)
    apart = one_hot((ri * WLON + cj) * 2 + lv, tok >= 0, TOK)
    loads[5].wait()
    for p in range(HALF):
        rows_f[2 * p : 2 * p + 2, :] = og[p].astype(F32)
    own_g[...] = nn(apart, rows_f[...].astype(BF)).astype(BF)
    pk_g[...] = nn(pack_ahead, own_g[...]).astype(BF)
    ge = send(pk_g, rl_g, C_GE, ahead)

    sel_own, sel_side, sel_far, edge_own, edge_side = roll_matrices(row_step, col_step, not late_col)
    edge_near = nn(edge_own, own_e[...])
    near = nn(sel_own, own_e[...])
    tq = iota((1, GT), 1)
    for k in range(1, GRP):
        tq = jnp.where(iota((1, GT), 1) >= k * TOK, iota((1, GT), 1) - k * TOK, tq)
    qri = split_token(tq)[1]
    first_wrapped = 16 * WLAT - s
    window_row = jnp.where(late_row, (lat + 15) % 16, lat) * WLAT
    wk = jnp.where(window_row + ri >= first_wrapped, 1, 0)
    wqv = jnp.where(window_row + qri >= first_wrapped, 1, 0)
    kk = iota((TOK, GT), 0)
    fold[...] = jnp.where(kk == tq, 1.0, 0.0).astype(BF)
    fh = lax.shift_right_logical(iota((GW, GT), 0), 5)
    lane_t = iota((GW, GT), 1)
    hmask[...] = jnp.where((lane_t >= fh * TOK) & (lane_t < (fh + 1) * TOK), 1.0, 0.0).astype(BF)
    group_head = lax.shift_right_logical(iota((TOK, GW), 1), 5)
    eye = jnp.where(iota((GW, GW), 0) == iota((GW, GW), 1), 1.0, 0.0).astype(BF)
    scale_rows = [
        lanes_of([stemp_ref[g * GRP + h] * SCALE for h in range(GRP)], (1, GT), 1, TOK) for g in range(2)
    ]
    n = iota((256, 1), 0)
    bit = lambda shift, mask: lax.shift_right_logical(n, shift) & mask
    wrow = bit(7, 1) * 256 + bit(4, 3) * 64 + core * 32 + bit(1, 7) * 4 + bit(6, 1) * 2 + (n & 1)
    pick = one_hot(wrow, n >= 0, D)

    ee.wait_recv()
    valid_1 = valid_of(rl_e) if late_col else kvp[...]
    sn_e[...] = with_valid(edge_near + nn(edge_side, rl_e[...]), valid_1)
    en = send_pair(sn_e, rn_e, C_EN, south, north)
    near = near + nn(sel_side, rl_e[...])
    ge.wait_recv()
    sn_g[...] = (nn(edge_own, own_g[...]) + nn(edge_side, rl_g[...])).astype(BF)
    gn = send_pair(sn_g, rn_g, C_GN, south, north)
    near_g = nn(sel_own, own_g[...]) + nn(sel_side, rl_g[...])
    back_own, back_side, back_far, bedge_own, bedge_side = roll_matrices(-row_step, -col_step, late_col)
    loads[3].wait()
    loads[4].wait()
    arrived(en)
    valid_2 = jnp.where(late_row, valid_of(rn_e), valid_1)
    lane = iota((TOK, 128), 1)
    valid_row = jnp.zeros((TOK, 128), F32)
    for r in range(WLAT):
        valid_row = jnp.where(ri == r, valid_2[r : r + 1, :128], valid_row)
    valid_k = jnp.sum(jnp.where(lane == cj, valid_row, 0.0), 1, keepdims=True)
    ok = (wk == wqv) & ((valid_k > 0.5) | (kk == tq))
    bias[...] = jnp.where(ok, 0.0, NEG)
    rolled = near + nn(sel_far, rn_e[...])

    mean = jnp.mean(rolled, 1, keepdims=True)
    centered = rolled - mean
    inv = lax.rsqrt(jnp.mean(centered * centered, 1, keepdims=True) + EPS)
    unit_v = centered * inv
    unit[...] = unit_v
    normed[...] = unit_v.astype(BF)
    tn = send(normed, m_normed, C_TN, mate)
    qkv[...] = nn(normed[...], wq[...]).astype(BF)
    for g in range(2):
        lanes = slice(g * GW, (g + 1) * GW)
        qg = qkv[:, g * GW : (g + 1) * GW]
        for h in range(GRP):
            qs[g, h * TOK : (h + 1) * TOK, :] = jnp.where(group_head == h, qg, jnp.zeros_like(qg))
        st = nt(qkv[:, D + g * GW : D + (g + 1) * GW], qs[g]) * scale_rows[g] + bias[...]
        e = jnp.exp(st - jnp.max(st, 0, keepdims=True))
        p = e * (1.0 / jnp.sum(e, 0, keepdims=True))
        pt[g] = p
        p16[g] = p.astype(BF)
        v_t = nt(eye, qkv[:, 2 * D + g * GW : 2 * D + (g + 1) * GW]).astype(BF)
        c_t = nn(v_t, p16[g]).astype(BF) * hmask[...]
        ctx[:, lanes] = nt(fold[...], c_t).astype(BF)
    tc = send(ctx, m_ctx, C_TC, mate)
    att[...] = nn(ctx[...], wo[...]).astype(BF)
    pk_a[...] = nn(pack_back, att[...]).astype(BF)
    aw = send(pk_a, rl_a, C_AW, back)

    arrived(gn)
    rgrad[...] = (near_g + nn(sel_far, rn_g[...])).astype(BF)
    tr = send(rgrad, m_rgrad, C_TR, mate)
    cgrad = nt(rgrad[...], wo[...]).astype(BF)
    for g in range(2):
        piece = cgrad[:, g * GW : (g + 1) * GW]
        for h in range(GRP):
            cgs[g, h * TOK : (h + 1) * TOK, :] = jnp.where(group_head == h, piece, jnp.zeros_like(piece))

    for g in range(2):
        vback[:, g * GW : (g + 1) * GW] = nn(p16[g], cgs[g]).astype(BF)
    tv = send(vback, m_vback, C_TV, mate)

    def scores_back(g):
        p = pt[g]
        dp = nt(qkv[:, 2 * D + g * GW : 2 * D + (g + 1) * GW], cgs[g])
        ds = p * (dp - jnp.sum(p * dp, 0, keepdims=True)) * scale_rows[g]
        ds16 = ds.astype(BF)
        k_t = nt(eye, qkv[:, D + g * GW : D + (g + 1) * GW]).astype(BF)
        q_t = nn(k_t, ds16).astype(BF) * hmask[...]
        qback[g, :, :GW] = nt(fold[...], q_t).astype(BF)
        qback[g, :, GW:] = nn(ds16, qs[g]).astype(BF)
        return send(qback.at[g], m_qback.at[g], C_TQ0 + g, mate)

    def picked(left, m_left):
        return nt(pick, left[...]).astype(BF), nt(pick, m_left[...]).astype(BF)

    def chip_sum(lefts, right, m_right):
        total = nn(lefts[0], right) + nn(lefts[1], m_right)
        return total.astype(BF).reshape(NY, NX, 16, right.shape[1])

    first_stage = []

    def share(low, width, first_a, first_b):
        lanes = pl.ds(low, width)
        for k in range(1, NY):
            src = send_a.at[(y + k) % NY, :, :, lanes]
            first_stage.append(send(src, r1a.at[k - 1, :, :, lanes], first_a + k - 1, y_peers[k - 1]))
        for k in range(1, NX):
            src = send_b.at[:, (x + k) % NX, :, lanes]
            first_stage.append(send(src, r1b.at[k - 1, :, :, lanes], first_b + k - 1, x_peers[k - 1]))

    tq0 = scores_back(0)
    tc.wait_recv()
    tr.wait_recv()
    g_out = chip_sum(picked(ctx, m_ctx), rgrad[...], m_rgrad[...])
    send_a[:, :, :, 768:] = g_out[:, :, :, :256]
    send_b[:, :, :, 768:] = g_out[:, :, :, 256:]
    tn.wait_recv()
    tv.wait_recv()
    lefts = picked(normed, m_normed)
    g_val = chip_sum(lefts, vback[...], m_vback[...])
    send_a[:, :, :, 512:768] = g_val[:, :, :, :256]
    send_b[:, :, :, 512:768] = g_val[:, :, :, 256:]
    share(512, 512, C_E1A, C_E1B)
    tq1 = scores_back(1)

    ugrad = nt(vback[...], wq[:, 2 * D :])
    for g in range(2):
        ugrad = ugrad + nt(qback[g, :, :GW], wq[:, g * GW : (g + 1) * GW])
        ugrad = ugrad + nt(qback[g, :, GW:], wq[:, D + g * GW : D + (g + 1) * GW])
    u = unit[...]
    xgrad = inv * (
        ugrad - jnp.mean(ugrad, 1, keepdims=True) - u * jnp.mean(ugrad * u, 1, keepdims=True)
    )
    xg[...] = xgrad.astype(BF)
    pk_x[...] = nn(pack_back, xg[...]).astype(BF)
    xw = send(pk_x, rl_x, C_XW, back)
    for g, copy, a1, b1 in ((0, tq0, C_M1A, C_M1B), (1, tq1, C_L1A, C_L1B)):
        copy.wait_recv()
        g_qk = chip_sum(lefts, qback[g], m_qback[g])
        send_a[:, :, :, g * GW : (g + 1) * GW] = g_qk[:, :, :, :GW]
        send_b[:, :, :, g * GW : (g + 1) * GW] = g_qk[:, :, :, GW:]
        share(g * GW, GW, a1, b1)
    near_x = own_g[...].astype(F32) + nn(back_own, xg[...])
    edge_x = nn(bedge_own, xg[...])
    aw.wait_recv()
    sn_a[...] = (nn(bedge_own, att[...]) + nn(bedge_side, rl_a[...])).astype(BF)
    near_a = nn(back_own, att[...]) + nn(back_side, rl_a[...])

    xw.wait_recv()
    sn_x[...] = (edge_x + nn(bedge_side, rl_x[...])).astype(BF)
    xs = send_pair(sn_x, rn_x, C_XS, south, north)
    near_x = near_x + nn(back_side, rl_x[...])
    as_ = send_pair(sn_a, rn_a, C_AS, south, north)
    for copy in first_stage:
        copy.wait_recv()
    sum_a = send_a[y].astype(F32)
    sum_b = send_b[:, x].astype(F32)
    for k in range(3):
        sum_a = sum_a + r1a[k].astype(F32)
        sum_b = sum_b + r1b[k].astype(F32)
    s2a[...] = sum_a.astype(BF)
    s2b[...] = sum_b.astype(BF)
    second_stage = []
    for k in range(1, NX):
        second_stage.append(send(s2a.at[(x + k) % NX], r2a.at[k - 1], C_2A + k - 1, x_peers[k - 1]))
    for k in range(1, NY):
        second_stage.append(send(s2b.at[(y + k) % NY], r2b.at[k - 1], C_2B + k - 1, y_peers[k - 1]))

    arrived(xs)
    egrad = (near_x + nn(back_far, rn_x[...])).astype(BF)

    cback[...] = nt(egrad, eo[...]).astype(BF).astype(F32)

    for p in range(HALF):
        rows = slice(p * PADL, (p + 1) * PADL)
        c0 = cback[p : p + 1, :]
        c1 = cback[HALF + p : HALF + p + 1, :]
        v = vals[rows, :].astype(F32)
        prod[rows, :D] = (c0 * v).astype(BF)
        prod[rows, D:] = (c1 * v).astype(BF)
        vgrad[rows, :] = (wexp[rows, :D].astype(F32) * c0 + wexp[rows, D:].astype(F32) * c1).astype(BF)

    key_q = nt(q_rows, kvw[:, :D]).astype(BF)
    for c in range(ROWS // CHUNK):
        rows = slice(c * CHUNK, (c + 1) * CHUNK)
        pg = nt(prod[rows, :], spread).reshape(CHUNK // PADL, PADL, 2 * HEADS)
        pm = prob[rows, :].reshape(CHUNK // PADL, PADL, 2 * HEADS)
        sg = pm * (pg - jnp.sum(pm * pg, 1, keepdims=True))
        prob[rows, :] = sg.reshape(CHUNK, 2 * HEADS) * lane_scale

    for copy in second_stage:
        copy.wait_recv()
    last_a = s2a[x].astype(F32)
    last_b = s2b[y].astype(F32)
    for k in range(3):
        last_a = last_a + r2a[k].astype(F32)
        last_b = last_b + r2b[k].astype(F32)
    for j in range(8):
        value = (last_a if j < 4 else last_b)[:, 256 * (j % 4) : 256 * (j % 4 + 1)]
        for h in range(2):
            s3f[h, pl.ds(j, 16, stride=8), :] = value[:, 128 * h : 128 * (h + 1)]
    for k in range(NZ):
        for h in range(2):
            s3[k, :, 128 * h : 128 * (h + 1)] = s3f[h, 16 * k : 16 * (k + 1), :].astype(BF)
    third_stage = []
    for k in range(1, NZ):
        third_stage.append(send(s3.at[(z + k) % NZ], r3.at[k - 1], C_3 + k - 1, z_peers[k - 1]))

    stores = []
    for c in range(ROWS // CHUNK):
        rows = slice(c * CHUNK, (c + 1) * CHUNK)
        lg = nt(vgrad[rows, :], kvw[:, D:]) + nn(prob[rows, :].astype(BF), key_q)
        patches = slice(c * CHUNK // PADL, (c + 1) * CHUNK // PADL)
        lg_v[patches] = lg.astype(BF).reshape(CHUNK // PADL, PADL, D)[:, :LEVELS, :]
        stores.append(pltpu.make_async_copy(lg_v.at[patches], lg_ref.at[patches], lsem.at[6 + c]))
        stores[-1].start()

    arrived(as_)
    out16 = (own_e[...].astype(F32) + (near_a + nn(back_far, rn_a[...]))).astype(BF)
    u_row = iota((TOK, 1), 0)
    together = one_hot((u_row & 1) * HALF + lax.shift_right_logical(u_row, 1), u_row >= 0, TOK)
    rows_f[...] = nn(together, out16)
    for p in range(HALF):
        out_v[p] = rows_f[2 * p : 2 * p + 2, :].astype(BF)
    stores.append(pltpu.make_async_copy(out_v, out_ref, lsem.at[9]))
    stores[-1].start()

    for copy in third_stage:
        copy.wait_recv()
    factor = GRAD_GAIN * (2 * 96 * 192) ** (-0.5)
    for h in range(2):
        total = s3f[h, pl.ds(pl.multiple_of(16 * z, 16), 16), :]
        for k in range(NZ - 1):
            total = total + r3[k, :, 128 * h : 128 * (h + 1)].astype(F32)
        total = total * factor
        for b in range(2):
            for j, row in ((0, 0), (1, 2), (4, 4), (5, 6), (2, 8), (6, 10)):
                at = 12 * b + row + h
                gq_ref[at : at + 1, :] = total[8 * b + j : 8 * b + j + 1, :]
            for j, row in ((3, 0), (7, 2)):
                at = 4 * b + row + h
                go_ref[at : at + 1, :] = total[8 * b + j : 8 * b + j + 1, :]
    for copy in started:
        copy.wait_send()
    for copy in stores:
        copy.wait()


def deliver(a, b, c, d, a_out, b_out, c_out, d_out, sems):
    pairs = ((a, a_out), (b, b_out), (c, c_out), (d, d_out))
    copies = [pltpu.make_async_copy(src, dst, sems.at[i]) for i, (src, dst) in enumerate(pairs)]
    for copy in copies:
        copy.start()
    for copy in copies:
        copy.wait()


def local(levels_in, latent_queries, enc_kv, enc_out, enc_temp, w_qkv, w_out, swin_temp, lat_shift, lon_shift, key_valid, output_grad):
    vmem = pl.BlockSpec(memory_space=pltpu.VMEM)
    smem = pl.BlockSpec(memory_space=pltpu.SMEM)
    hbm = pl.BlockSpec(memory_space=pl.ANY)
    V = pltpu.VMEM
    block = lambda rows: V((rows, D), BF)
    scratch = [
        V((HALF, LEVELS, D), BF), V((D, 2 * D), BF), V((D, D), BF), V((D, 3 * D), BF), V((D, D), BF), V((HALF, 2, D), BF),
        V((ROWS, D), BF),
        V((ROWS, D), BF),
        V((ROWS, 2 * HEADS), F32),
        V((ROWS, 2 * D), BF),
        V((ROWS, 2 * D), BF),
        V((ROWS, D), BF),
        V((8, 8 * HALF, 128), F32),
        V((TOK, D), F32),
        V((TOK, D), F32),
        V((8, D), F32),
        V((HALF, 2, D), BF),
        V((HALF, LEVELS, D), BF),
    ]
    for _ in range(4):
        scratch += [block(TOK), block(SIDE), block(SIDE), block(PAIR), block(PAIR)]
    scratch += [
        V((TOK, D), F32), V((TOK, 3 * D), BF), block(TOK), block(TOK), block(TOK), block(TOK), V((2, TOK, D), BF),
        block(TOK), block(TOK), block(TOK), block(TOK), V((2, TOK, D), BF),
        V((2, GT, GW), BF), V((2, GT, GW), BF), V((2, TOK, GT), F32), V((2, TOK, GT), BF),
        V((TOK, GT), F32), V((GW, GT), BF), V((TOK, GT), BF),
        V((NY, NX, 16, WIDE), BF), V((NY, NX, 16, WIDE), BF),
        V((3, NX, 16, WIDE), BF), V((3, NY, 16, WIDE), BF),
        V((NX, 16, WIDE), BF), V((NY, 16, WIDE), BF),
        V((3, 16, WIDE), BF), V((3, 16, WIDE), BF),
        V((2, 128, 128), F32), V((NZ, 16, 256), BF), V((NZ - 1, 16, 256), BF),
        pltpu.SemaphoreType.DMA((10,)),
        pltpu.SemaphoreType.DMA((N_COPY,)),
        pltpu.SemaphoreType.DMA((N_COPY,)),
    ]
    lev = jnp.transpose(levels_in, (1, 2, 0, 3)).reshape(HALF, LEVELS, D)
    og = jnp.transpose(output_grad, (1, 2, 0, 3)).reshape(HALF, 2, D)
    shapes = (
        jax.ShapeDtypeStruct((HALF, 2, D), BF),
        jax.ShapeDtypeStruct((HALF, LEVELS, D), BF),
        jax.ShapeDtypeStruct((24, 128), F32),
        jax.ShapeDtypeStruct((8, 128), F32),
    )

    def run(late_col):
        return pl.pallas_call(
            functools.partial(kernel, late_col),
            out_shape=shapes,
            in_specs=[hbm, vmem, hbm, hbm, smem, hbm, hbm, smem, smem, smem, vmem, hbm],
            out_specs=(hbm, hbm, vmem, vmem),
            scratch_shapes=scratch,
            compiler_params=pltpu.CompilerParams(
                collective_id=int(late_col), has_side_effects=True, vmem_limit_bytes=48 * 1024 * 1024
            ),
        )

    parts = lax.cond(
        lon_shift[0] > WLON // 2, run(True), run(False),
        lev, latent_queries, enc_kv, enc_out, enc_temp, w_qkv, w_out, swin_temp, lat_shift, lon_shift, key_valid, og,
    )
    out, lg, gq, go = pl.pallas_call(
        deliver,
        out_shape=shapes,
        in_specs=[hbm] * 4,
        out_specs=(hbm,) * 4,
        scratch_shapes=[pltpu.SemaphoreType.DMA((4,))],
    )(*parts)
    out = jnp.transpose(out.reshape(WLAT, WLON, 2, D), (2, 0, 1, 3))
    lg = jnp.transpose(lg.reshape(WLAT, WLON, LEVELS, D), (2, 0, 1, 3))
    return out, lg, gq.reshape(-1), go.reshape(-1)


def solution(mesh):
    return jax.shard_map(
        local,
        mesh=mesh,
        in_specs=(
            P(None, "lat", "lon", None), P(), P(), P(), P(), P(), P(), P(), P(), P(),
            P("lat", "lon"),
            P(None, "lat", "lon", None),
        ),
        out_specs=(
            P(None, "lat", "lon", None),
            P(None, "lat", "lon", None),
            P(("lat", "lon")),
            P(("lat", "lon")),
        ),
        check_vma=False,
    )
```

```python
import functools
import math

import jax
import jax.numpy as jnp
from jax import lax
from jax.experimental import pallas as pl
from jax.experimental.pallas import tpu as pltpu
from jax.sharding import PartitionSpec as P

MESH = pl.DeviceIdType.MESH
BF = jnp.bfloat16
F32 = jnp.float32

D = 512
HEADS = 16
HD = 32
LEVELS = 13
WLAT = 6
WLON = 12
PADL = 16
TOK = 2 * WLAT * WLON
HALF = WLAT * WLON
ROWS = HALF * PADL
CHUNK = 384
GRP = 8
GW = GRP * HD
GT = GRP * TOK
EPS = 1e-05
NEG = -1e30
GRAD_GAIN = 6.0
SCALE = 1.0 / math.sqrt(HD)

NY, NX, NZ = 4, 4, 8
WIDE = 1024
PIECES = ((0, 1, 2, 8, 9, 10, 12, 13), (4, 5, 3, 6, 7, 11, 14, 15))
EDGES = (0, 80, 128, 160, 240, 304)
PLACES = tuple(zip(EDGES[:-1], EDGES[1:]))
LON_AT, THREE_DIAG, TWO_DIAG, THREE_AT, TWO_AT, SIDES = EDGES
SIDES_1 = 160
FIRST = 40

(
    C_EE, C_GE, C_AW, C_XW, C_TN, C_TR, C_TC, C_TV, C_TQ0, C_TQ1, C_GN, C_AS, C_XS, C_1A, C_1B, C_2A, C_2B, C_3,
) = range(18)
N_COPY = 18
THREE, BOTH = 80, 144


def nt(a, b):
    return lax.dot_general(a, b, (((1,), (1,)), ((), ())), preferred_element_type=F32)


def nn(a, b):
    return lax.dot_general(a, b, (((1,), (0,)), ((), ())), preferred_element_type=F32)


def iota(shape, dim):
    return lax.broadcasted_iota(jnp.int32, shape, dim)


def split_token(t):
    level = (t >= HALF).astype(jnp.int32)
    rest = t - HALF * level
    row = lax.shift_right_logical(rest * 171, 11)
    return level, row, rest - row * WLON


def block_index(level, row, col, late_col):
    half = (col >= 6).astype(jnp.int32)
    return level * HALF + (1 - half if late_col else half) * 36 + row * 6 + col - 6 * half


def split_block(t, late_col):
    level = (t >= HALF).astype(jnp.int32)
    rest = t - HALF * level
    second = (rest >= 36).astype(jnp.int32)
    rest = rest - 36 * second
    row = lax.shift_right_logical(rest * 43, 8)
    return level, row, rest - 6 * row + 6 * (1 - second if late_col else second)


def window_index(level, row, col):
    return level * HALF + row * WLON + col


def split_part(u, rows, cols):
    size = rows * cols
    level = (u >= size).astype(jnp.int32)
    rest = u - size * level
    row = lax.shift_right_logical(rest * 171, 11) if cols == WLON else lax.shift_right_logical(rest * 43, 8)
    return level, row, rest - row * cols, u < 2 * size


def one_hot(index, keep, width):
    shape = (index.shape[0], width)
    return jnp.where(keep & (index == iota(shape, 1)), 1.0, 0.0).astype(BF)


def lon_pack(last_cols):
    level, row, col, real = split_part(iota((THREE, 1), 0), WLAT, 6)
    return one_hot(window_index(level, row, col + 6 * last_cols), real, TOK)


def block_packs(late_col):
    shapes = ((WLAT, 6, 0), (3, 6, 0), (2, 6, 4), (3, WLON, 0), (2, WLON, 4))
    first, rest = [], []
    for k, ((at, end), (rows, cols, r0)) in enumerate(zip(PLACES, shapes)):
        level, row, col, real = split_part(iota((end - at, 1), 0), rows, cols)
        if k < 3:
            first.append(one_hot(level * FIRST + (row + r0) * 6 + col, real, 2 * FIRST))
        else:
            rest.append(one_hot(block_index(level, row + r0, col, late_col), real, TOK))
    return jnp.concatenate(first, 0), jnp.concatenate(rest, 0)


def roll_matrices(row_step, col_step, last_cols):
    lv, ri, cj = split_token(iota((TOK, 1), 0))
    row, col = ri + row_step, cj + col_step
    row_in = (row >= 0) & (row < WLAT)
    col_in = (col >= 0) & (col < WLON)
    own = one_hot(block_index(lv, row, col, last_cols), row_in & col_in, TOK)
    far_col = col + (WLON // 2 if last_cols else -WLON)
    over = row >= WLAT
    far_row = jnp.where(over, row - WLAT, row + 2)
    line = far_row * WLON + col
    corner = far_row * 6 + far_col
    lon = LON_AT + lv * 36 + row * 6 + far_col
    lat = jnp.where(over, THREE_AT + lv * 36 + line, TWO_AT + lv * 24 + line)
    diag = jnp.where(over, THREE_DIAG + lv * 18 + corner, TWO_DIAG + lv * 12 + corner)
    side = jnp.where(row_in, lon, jnp.where(col_in, lat, diag))
    return own, one_hot(side, ~(row_in & col_in), SIDES)


def two_step_matrices(row_step, col_step, three_last, last_cols, place, index):
    def along_lon(level, row, col, keep):
        inside = (col >= 0) & (col < WLON)
        own = one_hot(index(level, row, col), keep & inside, TOK)
        far_col = col + (WLON // 2 if last_cols else -WLON)
        return own, one_hot(level * 36 + row * 6 + far_col, keep & (~inside), THREE)

    lv, ri, cj = place(iota((TOK, 1), 0))
    row = ri + row_step
    row_in = (row >= 0) & (row < WLAT)
    own, side = along_lon(lv, row, cj + col_step, row_in)
    over = row >= WLAT
    line = jnp.where(over, row - WLAT, row + (3 if three_last else 2)) * WLON + cj
    in_three = ~over if three_last else over
    far = one_hot(jnp.where(in_three, lv * 36 + line, THREE + lv * 24 + line), ~row_in, BOTH)
    edges = []
    for length, rows, first in ((THREE, 3, 3 if three_last else 0), (BOTH - THREE, 2, 0 if three_last else 4)):
        level, row, col, real = split_part(iota((length, 1), 0), rows, WLON)
        edges.append(along_lon(level, row + first, col + col_step, real))
    edge_own, edge_side = (jnp.concatenate([e[i] for e in edges], 0) for i in range(2))
    return own, side, far, edge_own, edge_side


def lanes_of(values, shape, dim, step):
    index = iota(shape, dim)
    out = jnp.zeros(shape, F32)
    for k, v in enumerate(values):
        out = jnp.where((index >= k * step) & (index < (k + 1) * step), v, out)
    return out


def kernel(
    late_col,
    lev_hbm, q_hbm, kvw_hbm, eo_hbm, etemp_hbm, wq_hbm, wo_hbm, stemp_hbm, lats_hbm, lons_hbm, valid_hbm, og_hbm,
    out_hbm, lg_hbm, gq_hbm, go_hbm,
    lev, kvw, eo, wq, wo, og, q_ref, etemp_ref, stemp_ref, lats_ref, lons_ref, valid_ref,
    levp, vals, prob, wexp, prod, vgrad, part, cback, rows_f, kvp, out_v, lg_v, gq_ref, go_ref,
    own_e, pk_e, rl_e,
    own_g, pk_g, rl_g, sn_g, rn_g,
    att, pk_a, rl_a, sn_a, rn_a,
    xg, pk_x, rl_x, sn_x, rn_x,
    unit, qkv, normed, rgrad, ctx, qgrad,
    m_normed, m_rgrad, m_ctx, m_qgrad,
    qs, cgs, pt, p16, bias, hmask, fold,
    send_a, send_b, r1a, r1b, s2a, s2b, r2a, r2b, s3f, s3, r3,
    lsem, ssem, rsem,
):
    lat = lax.axis_index("lat")
    lon = lax.axis_index("lon")
    y_hi = lat // 8
    x = (lat // 2) % 4
    core = lat % 2
    z = lon // 2
    y_lo = lon % 2
    y = y_hi * 2 + y_lo

    def device(yy, xx, cc, zz):
        return ((yy // 2) * 8 + xx * 2 + cc, zz * 2 + yy % 2)

    mate = (lat + 1 - 2 * core, lon)
    east = (lat, (lon + 1) % 16)
    west = (lat, (lon + 15) % 16)
    north = ((lat + 1) % 16, lon)
    south = ((lat + 15) % 16, lon)
    y_peers = [device((y + k) % NY, x, core, z) for k in range(1, NY)]
    x_peers = [device(y, (x + k) % NX, core, z) for k in range(1, NX)]
    z_peers = [device(y, x, core, (z + k) % NZ) for k in range(1, NZ)]
    lon_ahead, lon_back = (east, west) if late_col else (west, east)
    ahead = (lon_ahead, (south[0], lon_ahead[1]), (north[0], lon_ahead[1]), south, north)
    greeted = [mate, *ahead, lon_back, (north[0], lon_back[1]), (south[0], lon_back[1])] + y_peers + x_peers + z_peers
    barrier = pltpu.get_barrier_semaphore()
    for peer in greeted:
        pl.semaphore_signal(barrier, inc=1, device_id=peer, device_id_type=MESH)

    loads = []

    def load(src, dst):
        loads.append(pltpu.make_async_copy(src, dst, lsem.at[len(loads)]))
        loads[-1].start()
        return loads[-1]

    small = [
        load(src, dst)
        for src, dst in (
            (lats_hbm, lats_ref), (lons_hbm, lons_ref), (valid_hbm, valid_ref), (q_hbm, q_ref),
            (etemp_hbm, etemp_ref), (stemp_hbm, stemp_ref),
        )
    ]
    load_og = load(og_hbm, og)
    load_kvw = load(kvw_hbm, kvw)
    load_lev = load(lev_hbm, lev)
    landings = {}

    def send(src, dst, index, peer, landing=None):
        landings[index] = dst if landing is None else landing
        pltpu.make_async_remote_copy(
            src_ref=src, dst_ref=dst, send_sem=ssem.at[index], recv_sem=rsem.at[index],
            device_id=peer, device_id_type=MESH,
        ).start()

    def whole(index):
        return pltpu.make_async_remote_copy(
            src_ref=landings[index], dst_ref=landings[index], send_sem=ssem.at[index], recv_sem=rsem.at[index],
            device_id=mate, device_id_type=MESH,
        )

    def arrived(index):
        whole(index).wait_recv()

    def send_sides(places, peers):
        for (at, end), peer in zip(places, peers):
            part_of = pl.ds(at, end - at)
            send(pk_e.at[part_of], rl_e.at[part_of], C_EE, peer, rl_e)

    def send_lat(src, dst, index, three_to, two_to):
        for part_of, peer in ((pl.ds(0, THREE), three_to), (pl.ds(THREE, BOTH - THREE), two_to)):
            send(src.at[part_of], dst.at[part_of], index, peer, dst)

    pack_first, pack_rest = block_packs(late_col)
    pack_back = lon_pack(not late_col)
    tok = iota((TOK, 1), 0)
    lv, ri, cj = split_token(tok)
    own_index = functools.partial(block_index, late_col=late_col)
    own_place = functools.partial(split_block, late_col=late_col)
    olv, ori, ocj = own_place(tok)
    apart = one_hot((ori * WLON + ocj) * 2 + olv, tok >= 0, TOK)
    load_og.wait()
    for p in range(HALF):
        rows_f[2 * p : 2 * p + 2, :] = og[p].astype(F32)
    own_g[...] = nn(apart, rows_f[...].astype(BF)).astype(BF)
    glv, gri, gcj, greal = split_part(iota((THREE, 1), 0), WLAT, 6)
    pk_g[...] = nn(one_hot(glv * HALF + gri * 6 + gcj, greal, TOK), own_g[...]).astype(BF)
    pl.semaphore_wait(barrier, len(greeted))
    send(pk_g, rl_g, C_GE, lon_ahead)
    for copy in small:
        copy.wait()
    s = lats_ref[0]
    t = lons_ref[0]
    late_row = s > WLAT // 2
    row_step = jnp.where(late_row, s - WLAT, s)
    col_step = t - WLON if late_col else t
    sel_own, sel_side = roll_matrices(row_step, col_step, late_col)
    kvp[...] = jnp.zeros((8, D), F32)
    kvp[0:WLAT, 0:WLON] = valid_ref[...].astype(F32)

    def with_valid(sides, places):
        pieces, base = [], places[0][0]
        for at, end in places:
            pieces += [sides[at - base : end - base - 8], kvp[...]]
        return jnp.concatenate(pieces, 0).astype(BF)

    q_rows = jnp.concatenate([jnp.broadcast_to(q_ref[l : l + 1, :], (HEADS, D)) for l in range(2)], 0)
    row_head = iota((2 * HEADS, D), 0) % HEADS
    lane_head = lax.shift_right_logical(iota((2 * HEADS, D), 1), 5)
    q_rows = jnp.where(row_head == lane_head, q_rows.astype(F32), 0.0).astype(BF)
    lane_scale = lanes_of([etemp_ref[h] * SCALE for h in range(HEADS)] * 2, (1, 2 * HEADS), 1, 1)
    load_kvw.wait()
    load_lev.wait()
    load_eo = load(eo_hbm, eo)
    load_wo = load(wo_hbm, wo)
    wq_sem = lsem.at[len(loads)]
    for src, dst, width in ((0, 0, GW), (D, GW, GW), (GW, D, GW), (D + GW, D + GW, GW), (2 * D, 2 * D, D)):
        pltpu.make_async_copy(wq_hbm.at[:, pl.ds(src, width)], wq.at[:, pl.ds(dst, width)], wq_sem).start()
    filler = jnp.zeros((6, PADL - LEVELS, D), BF)

    def run_of(k):
        return 12 * (k % WLAT) + 6 * ((k // WLAT) ^ int(late_col))

    for k in range(2 * WLAT):
        block = jnp.concatenate([lev[run_of(k) : run_of(k) + 6], filler], 1)
        levp[6 * PADL * k : 6 * PADL * (k + 1), :] = block.reshape(6 * PADL, D)
    spread_row = iota((2 * HEADS, 2 * D), 0)
    spread = jnp.where(lax.shift_right_logical(iota((2 * HEADS, 2 * D), 1), 5) == spread_row, 1.0, 0.0).astype(BF)

    def encode_rows(low, high):
        rows, count = slice(low, high), (high - low) // PADL
        kv = nn(levp[rows, :], kvw[...])
        vals[rows, :] = kv[:, D:].astype(BF)
        sc = (nt(kv[:, :D].astype(BF), q_rows) * lane_scale).reshape(count, PADL, 2 * HEADS)
        sc = jnp.where(iota((count, PADL, 2 * HEADS), 1) < LEVELS, sc, NEG)
        e = jnp.exp(sc - jnp.max(sc, 1, keepdims=True))
        pm = e * (1.0 / jnp.sum(e, 1, keepdims=True))
        prob[rows, :] = pm.reshape(high - low, 2 * HEADS)

    def context_of(c):
        rows = slice(8 * PADL * c, 8 * PADL * (c + 1))
        w = nn(prob[rows, :].astype(BF), spread)
        wexp[rows, :] = w.astype(BF)
        v = vals[rows, :].astype(F32)
        for l in range(2):
            product = (w[:, l * D : (l + 1) * D] * v).reshape(8, 2, 8, D)
            product = (product[:, 0] + product[:, 1]).reshape(64, D)
            for j in range(4):
                part[4 * l + j, 64 * c : 64 * (c + 1), :] = product[:, 128 * j : 128 * (j + 1)]
        for l in range(2):
            for j in range(4):
                acc = part[4 * l + j, pl.ds(64 * c, 8, stride=8), :]
                for m in range(1, 8):
                    acc = acc + part[4 * l + j, pl.ds(64 * c + m, 8, stride=8), :]
                cback[l * HALF + 8 * c : l * HALF + 8 * (c + 1), 128 * j : 128 * (j + 1)] = acc

    def encoded_of(low, high):
        count = high - low
        context = jnp.concatenate([cback[low:high, :], cback[HALF + low : HALF + high, :]], 0)
        mixed = nn(context.astype(BF), eo[...])
        second = iota((2 * count, D), 0) >= count
        query = jnp.where(second, q_ref[1:2, :].astype(F32), q_ref[0:1, :].astype(F32))
        result = (query + mixed).astype(BF)
        for l in range(2):
            rows_f[l * HALF + low : l * HALF + high, :] = result[l * count : (l + 1) * count].astype(F32)
        return result

    encode_rows(0, 320)
    encode_rows(320, 640)
    for c in range(FIRST // 8):
        context_of(c)
    load_eo.wait()
    pk_e[:SIDES_1, :] = with_valid(nn(pack_first, encoded_of(0, FIRST)), PLACES[:3])
    send_sides(PLACES[:3], ahead[:3])
    encode_rows(640, 896)
    encode_rows(896, 1152)
    for c in range(FIRST // 8, HALF // 8):
        context_of(c)
    encoded_of(FIRST, HALF)
    own_e[...] = rows_f[...].astype(BF)
    pk_e[SIDES_1:, :] = with_valid(nn(pack_rest, own_e[...]), PLACES[3:])
    send_sides(PLACES[3:], ahead[3:])
    near = nn(sel_own, own_e[...])
    two_own, two_side, two_far, two_edge_own, two_edge_side = two_step_matrices(
        row_step, col_step, False, late_col, split_token, own_index
    )
    near_g = nn(two_own, own_g[...])
    edge_g = nn(two_edge_own, own_g[...])
    arrived(C_GE)
    sn_g[...] = (edge_g + nn(two_edge_side, rl_g[...])).astype(BF)
    send_lat(sn_g, rn_g, C_GN, south, north)
    near_g = near_g + nn(two_side, rl_g[...])
    tq = iota((1, GT), 1)
    for k in range(1, GRP):
        tq = jnp.where(iota((1, GT), 1) >= k * TOK, iota((1, GT), 1) - k * TOK, tq)
    qri = split_token(tq)[1]
    first_wrapped = 16 * WLAT - s
    window_row = jnp.where(late_row, (lat + 15) % 16, lat) * WLAT
    wk = jnp.where(window_row + ri >= first_wrapped, 1, 0)
    wqv = jnp.where(window_row + qri >= first_wrapped, 1, 0)
    kk = iota((TOK, GT), 0)
    fold[...] = jnp.where(kk == tq, 1.0, 0.0).astype(BF)
    fh = lax.shift_right_logical(iota((GW, GT), 0), 5)
    lane_t = iota((GW, GT), 1)
    hmask[...] = jnp.where((lane_t >= fh * TOK) & (lane_t < (fh + 1) * TOK), 1.0, 0.0).astype(BF)
    group_head = lax.shift_right_logical(iota((TOK, GW), 1), 5)
    eye = jnp.where(iota((GW, GW), 0) == iota((GW, GW), 1), 1.0, 0.0).astype(BF)
    scale_rows = [
        lanes_of([stemp_ref[g * GRP + h] * SCALE for h in range(GRP)], (1, GT), 1, TOK) for g in range(2)
    ]
    n = iota((256, 1), 0)
    bit = lambda shift, mask: lax.shift_right_logical(n, shift) & mask
    wrow = bit(7, 1) * 256 + bit(4, 3) * 64 + core * 32 + bit(1, 7) * 4 + bit(6, 1) * 2 + (n & 1)
    pick = one_hot(wrow, n >= 0, D)

    back_own, back_side, back_far, bedge_own, bedge_side = two_step_matrices(
        -row_step, -col_step, True, not late_col, own_place, window_index
    )
    pltpu.make_async_copy(wq_hbm, wq, wq_sem).wait()
    arrived(C_EE)
    beside = rl_e[THREE_DIAG - 8 : THREE_DIAG, :].astype(F32) if late_col else kvp[...]
    end = THREE_AT if late_col else SIDES
    valid_2 = jnp.where(late_row, rl_e[end - 8 : end, :].astype(F32), beside)
    lane = iota((TOK, 128), 1)
    valid_row = jnp.zeros((TOK, 128), F32)
    for r in range(WLAT):
        valid_row = jnp.where(ri == r, valid_2[r : r + 1, :128], valid_row)
    valid_k = jnp.sum(jnp.where(lane == cj, valid_row, 0.0), 1, keepdims=True)
    ok = (wk == wqv) & ((valid_k > 0.5) | (kk == tq))
    bias[...] = jnp.where(ok, 0.0, NEG)
    rolled = near + nn(sel_side, rl_e[...])

    mean = jnp.mean(rolled, 1, keepdims=True)
    centered = rolled - mean
    inv = lax.rsqrt(jnp.mean(centered * centered, 1, keepdims=True) + EPS)
    unit_v = centered * inv
    unit[...] = unit_v
    normed[...] = unit_v.astype(BF)
    send(normed, m_normed, C_TN, mate)
    qkv[...] = nn(normed[...], wq[...]).astype(BF)
    for g in range(2):
        lanes = slice(g * GW, (g + 1) * GW)
        qg = qkv[:, g * D : g * D + GW]
        for h in range(GRP):
            qs[g, h * TOK : (h + 1) * TOK, :] = jnp.where(group_head == h, qg, jnp.zeros_like(qg))
        st = nt(qkv[:, g * D + GW : (g + 1) * D], qs[g]) * scale_rows[g] + bias[...]
        e = jnp.exp(st - jnp.max(st, 0, keepdims=True))
        p = e * (1.0 / jnp.sum(e, 0, keepdims=True))
        pt[g] = p
        p16[g] = p.astype(BF)
        v_t = nt(eye, qkv[:, 2 * D + g * GW : 2 * D + (g + 1) * GW]).astype(BF)
        c_t = nn(v_t, p16[g]).astype(BF) * hmask[...]
        ctx[:, lanes] = nt(fold[...], c_t).astype(BF)
    send(ctx, m_ctx, C_TC, mate)
    load_wo.wait()
    att[...] = nn(ctx[...], wo[...]).astype(BF)
    pk_a[...] = nn(pack_back, att[...]).astype(BF)
    send(pk_a, rl_a, C_AW, lon_back)

    arrived(C_GN)
    rgrad[...] = (near_g + nn(two_far, rn_g[...])).astype(BF)
    send(rgrad, m_rgrad, C_TR, mate)
    cgrad = nt(rgrad[...], wo[...]).astype(BF)
    for g in range(2):
        piece = cgrad[:, g * GW : (g + 1) * GW]
        for h in range(GRP):
            cgs[g, h * TOK : (h + 1) * TOK, :] = jnp.where(group_head == h, piece, jnp.zeros_like(piece))
    for g in range(2):
        qgrad[:, 2 * D + g * GW : 2 * D + (g + 1) * GW] = nn(p16[g], cgs[g]).astype(BF)
    third = [pl.ds(k * D, D) for k in range(3)]
    send(qgrad.at[:, third[2]], m_qgrad.at[:, third[2]], C_TV, mate)

    def scores_back(g):
        p = pt[g]
        dp = nt(qkv[:, 2 * D + g * GW : 2 * D + (g + 1) * GW], cgs[g])
        ds = p * (dp - jnp.sum(p * dp, 0, keepdims=True)) * scale_rows[g]
        ds16 = ds.astype(BF)
        k_t = nt(eye, qkv[:, g * D + GW : (g + 1) * D]).astype(BF)
        q_t = nn(k_t, ds16).astype(BF) * hmask[...]
        qgrad[:, g * D : g * D + GW] = nt(fold[...], q_t).astype(BF)
        qgrad[:, g * D + GW : (g + 1) * D] = nn(ds16, qs[g]).astype(BF)
        send(qgrad.at[:, third[g]], m_qgrad.at[:, third[g]], C_TQ0 + g, mate)

    def picked(left, m_left):
        return nt(pick, left[...]).astype(BF), nt(pick, m_left[...]).astype(BF)

    def chip_sum(lefts, right, m_right):
        total = nn(lefts[0], right) + nn(lefts[1], m_right)
        return total.astype(BF).reshape(NY, NX, 16, right.shape[1])

    def share(low_a, width_a, low_b, width_b):
        a, b = pl.ds(low_a, width_a), pl.ds(low_b, width_b)
        for k in range(1, NY):
            send(send_a.at[(y + k) % NY, :, :, a], r1a.at[k - 1, :, :, a], C_1A, y_peers[k - 1], r1a)
        for k in range(1, NX):
            send(send_b.at[:, (x + k) % NX, :, b], r1b.at[k - 1, :, :, b], C_1B, x_peers[k - 1], r1b)

    arrived(C_TC)
    arrived(C_TR)
    g_out = chip_sum(picked(ctx, m_ctx), rgrad[...], m_rgrad[...])
    send_a[:, :, :, 768:] = g_out[:, :, :, :256]
    send_b[:, :, :, 768:] = g_out[:, :, :, 256:]
    share(768, 256, 768, 256)
    scores_back(0)
    arrived(C_TN)
    arrived(C_TV)
    lefts = picked(normed, m_normed)
    g_val = chip_sum(lefts, qgrad[:, 2 * D :], m_qgrad[:, 2 * D :])
    send_a[:, :, :, 384:768] = g_val[:, :, :, :384]
    send_b[:, :, :, 640:768] = g_val[:, :, :, 384:]
    share(384, 384, 640, 128)
    scores_back(1)

    def sum_qk(g):
        arrived(C_TQ0 + g)
        return chip_sum(lefts, qgrad[:, g * D : (g + 1) * D], m_qgrad[:, g * D : (g + 1) * D])

    g_qk = sum_qk(0)
    send_a[:, :, :, :256] = g_qk[:, :, :, :256]
    send_b[:, :, :, :256] = g_qk[:, :, :, 256:]
    share(0, 256, 0, 256)
    ugrad = nt(qgrad[...], wq[...])
    u = unit[...]
    xgrad = inv * (
        ugrad - jnp.mean(ugrad, 1, keepdims=True) - u * jnp.mean(ugrad * u, 1, keepdims=True)
    )
    xg[...] = xgrad.astype(BF)
    pk_x[...] = nn(pack_back, xg[...]).astype(BF)
    send(pk_x, rl_x, C_XW, lon_back)
    g_qk = sum_qk(1)
    send_a[:, :, :, 256:384] = g_qk[:, :, :, :128]
    send_b[:, :, :, 256:640] = g_qk[:, :, :, 128:]
    share(256, 128, 256, 384)
    near_x = own_g[...].astype(F32) + nn(back_own, xg[...])
    key_q = nt(q_rows, kvw[:, :D]).astype(BF)
    edge_x = nn(bedge_own, xg[...])
    arrived(C_AW)
    sn_a[...] = (nn(bedge_own, att[...]) + nn(bedge_side, rl_a[...])).astype(BF)
    near_a = nn(back_own, att[...]) + nn(back_side, rl_a[...])
    arrived(C_XW)
    sn_x[...] = (edge_x + nn(bedge_side, rl_x[...])).astype(BF)
    send_lat(sn_x, rn_x, C_XS, north, south)
    near_x = near_x + nn(back_side, rl_x[...])
    arrived(C_1A)
    arrived(C_1B)
    sum_a = send_a[y].astype(F32)
    sum_b = send_b[:, x].astype(F32)
    for k in range(3):
        sum_a = sum_a + r1a[k].astype(F32)
        sum_b = sum_b + r1b[k].astype(F32)
    s2a[...] = sum_a.astype(BF)
    s2b[...] = sum_b.astype(BF)
    for k in range(1, NX):
        send(s2a.at[(x + k) % NX], r2a.at[k - 1], C_2A, x_peers[k - 1], r2a)
    for k in range(1, NY):
        send(s2b.at[(y + k) % NY], r2b.at[k - 1], C_2B, y_peers[k - 1], r2b)
    arrived(C_XS)
    send_lat(sn_a, rn_a, C_AS, north, south)
    egrad = (near_x + nn(back_far, rn_x[...])).astype(BF)

    cback[...] = nt(egrad, eo[...]).astype(BF).astype(F32)

    for p in range(HALF):
        rows = slice(p * PADL, (p + 1) * PADL)
        c0 = cback[p : p + 1, :]
        c1 = cback[HALF + p : HALF + p + 1, :]
        v = vals[rows, :].astype(F32)
        prod[rows, :D] = (c0 * v).astype(BF)
        prod[rows, D:] = (c1 * v).astype(BF)
        vgrad[rows, :] = (wexp[rows, :D].astype(F32) * c0 + wexp[rows, D:].astype(F32) * c1).astype(BF)

    for c in range(ROWS // CHUNK):
        rows = slice(c * CHUNK, (c + 1) * CHUNK)
        pg = nt(prod[rows, :], spread).reshape(CHUNK // PADL, PADL, 2 * HEADS)
        pm = prob[rows, :].reshape(CHUNK // PADL, PADL, 2 * HEADS)
        sg = pm * (pg - jnp.sum(pm * pg, 1, keepdims=True))
        prob[rows, :] = sg.reshape(CHUNK, 2 * HEADS) * lane_scale

    def level_grads(c):
        rows = slice(c * CHUNK, (c + 1) * CHUNK)
        lg = nt(vgrad[rows, :], kvw[:, D:]) + nn(prob[rows, :].astype(BF), key_q)
        lg = lg.astype(BF).reshape(CHUNK // PADL, PADL, D)
        for k in range(4):
            lg_v[run_of(4 * c + k) : run_of(4 * c + k) + 6] = lg[6 * k : 6 * (k + 1), :LEVELS, :]

    arrived(C_2A)
    arrived(C_2B)
    last_a = s2a[x].astype(F32)
    last_b = s2b[y].astype(F32)
    for k in range(3):
        last_a = last_a + r2a[k].astype(F32)
        last_b = last_b + r2b[k].astype(F32)
    for j in range(8):
        value = (last_a if j < 4 else last_b)[:, 256 * (j % 4) : 256 * (j % 4 + 1)]
        for h in range(2):
            s3f[h, pl.ds(j, 16, stride=8), :] = value[:, 128 * h : 128 * (h + 1)]
    for k in range(NZ):
        for h in range(2):
            s3[k, :, 128 * h : 128 * (h + 1)] = s3f[h, 16 * k : 16 * (k + 1), :].astype(BF)
    for k in range(1, NZ):
        send(s3.at[(z + k) % NZ], r3.at[k - 1], C_3, z_peers[k - 1], r3)

    for c in range(3):
        level_grads(c)
    stores = [pltpu.make_async_copy(lg_v, lg_hbm, lsem.at[len(loads) + 1])]
    stores[-1].start()
    arrived(C_AS)
    added = near_a + nn(back_far, rn_a[...])
    out16 = (own_e[...].astype(F32) + added).astype(BF)
    u_row = iota((TOK, 1), 0)
    u_patch = lax.shift_right_logical(u_row, 1)
    u_lat = lax.shift_right_logical(u_patch * 171, 11)
    together = one_hot(own_index(u_row & 1, u_lat, u_patch - u_lat * WLON), u_row >= 0, TOK)
    rows_f[...] = nn(together, out16)
    for p in range(HALF):
        out_v[p] = rows_f[2 * p : 2 * p + 2, :].astype(BF)
    stores.append(pltpu.make_async_copy(out_v, out_hbm, lsem.at[len(loads) + 2]))
    stores[-1].start()

    arrived(C_3)
    factor = GRAD_GAIN * (2 * 96 * 192) ** (-0.5)
    for h in range(2):
        total = s3f[h, pl.ds(pl.multiple_of(16 * z, 16), 16), :]
        for k in range(NZ - 1):
            total = total + r3[k, :, 128 * h : 128 * (h + 1)].astype(F32)
        total = total * factor
        for b in range(2):
            for j in range(8):
                piece = total[8 * b + j : 8 * b + j + 1, :]
                place = PIECES[j // 4][2 * (j % 4) + h]
                if place < 12:
                    gq_ref[12 * b + place : 12 * b + place + 1, :] = piece
                else:
                    go_ref[4 * b + place - 12 : 4 * b + place - 11, :] = piece
    for i, (src, dst) in enumerate(((gq_ref, gq_hbm), (go_ref, go_hbm))):
        stores.append(pltpu.make_async_copy(src, dst, lsem.at[len(loads) + 3 + i]))
        stores[-1].start()
    for index in landings:
        whole(index).wait_send()
    for copy in stores:
        copy.wait()


def deliver(a, b, c, d, a_out, b_out, c_out, d_out, sems):
    pairs = ((a, a_out), (b, b_out), (c, c_out), (d, d_out))
    copies = [pltpu.make_async_copy(src, dst, sems.at[i]) for i, (src, dst) in enumerate(pairs)]
    for copy in copies:
        copy.start()
    for copy in copies:
        copy.wait()


def local(levels_in, latent_queries, enc_kv, enc_out, enc_temp, w_qkv, w_out, swin_temp, lat_shift, lon_shift, key_valid, output_grad):
    hbm = pl.BlockSpec(memory_space=pl.ANY)
    V = pltpu.VMEM
    block = lambda rows: V((rows, D), BF)
    scratch = [
        V((HALF, LEVELS, D), BF), V((D, 2 * D), BF), V((D, D), BF), V((D, 3 * D), BF), V((D, D), BF), V((HALF, 2, D), BF),
        V((2, D), BF), pltpu.SMEM((HEADS,), F32), pltpu.SMEM((HEADS,), F32), pltpu.SMEM((1,), jnp.int32),
        pltpu.SMEM((1,), jnp.int32), V((WLAT, WLON), jnp.int32),
        V((ROWS, D), BF),
        V((ROWS, D), BF),
        V((ROWS, 2 * HEADS), F32),
        V((ROWS, 2 * D), BF),
        V((ROWS, 2 * D), BF),
        V((ROWS, D), BF),
        V((8, 8 * HALF, 128), F32),
        V((TOK, D), F32),
        V((TOK, D), F32),
        V((8, D), F32),
        V((HALF, 2, D), BF),
        V((HALF, LEVELS, D), BF),
        V((24, 128), F32), V((8, 128), F32),
    ]
    scratch += [block(TOK), block(SIDES), block(SIDES)]
    for _ in range(3):
        scratch += [block(TOK), block(THREE), block(THREE), block(BOTH), block(BOTH)]
    scratch += [
        V((TOK, D), F32), V((TOK, 3 * D), BF), block(TOK), block(TOK), block(TOK), V((TOK, 3 * D), BF),
        block(TOK), block(TOK), block(TOK), V((TOK, 3 * D), BF),
        V((2, GT, GW), BF), V((2, GT, GW), BF), V((2, TOK, GT), F32), V((2, TOK, GT), BF),
        V((TOK, GT), F32), V((GW, GT), BF), V((TOK, GT), BF),
        V((NY, NX, 16, WIDE), BF), V((NY, NX, 16, WIDE), BF),
        V((3, NX, 16, WIDE), BF), V((3, NY, 16, WIDE), BF),
        V((NX, 16, WIDE), BF), V((NY, 16, WIDE), BF),
        V((3, 16, WIDE), BF), V((3, 16, WIDE), BF),
        V((2, 128, 128), F32), V((NZ, 16, 256), BF), V((NZ - 1, 16, 256), BF),
        pltpu.SemaphoreType.DMA((16,)),
        pltpu.SemaphoreType.DMA((N_COPY,)),
        pltpu.SemaphoreType.DMA((N_COPY,)),
    ]
    lev = jnp.transpose(levels_in, (1, 2, 0, 3)).reshape(HALF, LEVELS, D)
    og = jnp.transpose(output_grad, (1, 2, 0, 3)).reshape(HALF, 2, D)
    shapes = (
        jax.ShapeDtypeStruct((HALF, 2, D), BF),
        jax.ShapeDtypeStruct((HALF, LEVELS, D), BF),
        jax.ShapeDtypeStruct((24, 128), F32),
        jax.ShapeDtypeStruct((8, 128), F32),
    )

    def run(late_col):
        return pl.pallas_call(
            functools.partial(kernel, late_col),
            out_shape=shapes,
            in_specs=[hbm] * 12,
            out_specs=(hbm,) * 4,
            scratch_shapes=scratch,
            compiler_params=pltpu.CompilerParams(
                collective_id=int(late_col), has_side_effects=True, vmem_limit_bytes=48 * 1024 * 1024
            ),
        )

    parts = lax.cond(
        lon_shift[0] > WLON // 2, run(True), run(False),
        lev, latent_queries, enc_kv, enc_out, enc_temp, w_qkv, w_out, swin_temp, lat_shift, lon_shift, key_valid, og,
    )
    out, lg, gq, go = pl.pallas_call(
        deliver,
        out_shape=shapes,
        in_specs=[hbm] * 4,
        out_specs=(hbm,) * 4,
        scratch_shapes=[pltpu.SemaphoreType.DMA((4,))],
    )(*parts)
    out = jnp.transpose(out.reshape(WLAT, WLON, 2, D), (2, 0, 1, 3))
    lg = jnp.transpose(lg.reshape(WLAT, WLON, LEVELS, D), (2, 0, 1, 3))
    return out, lg, gq.reshape(-1), go.reshape(-1)


def solution(mesh):
    return jax.shard_map(
        local,
        mesh=mesh,
        in_specs=(
            P(None, "lat", "lon", None), P(), P(), P(), P(), P(), P(), P(), P(), P(),
            P("lat", "lon"),
            P(None, "lat", "lon", None),
        ),
        out_specs=(
            P(None, "lat", "lon", None),
            P(None, "lat", "lon", None),
            P(("lat", "lon")),
            P(("lat", "lon")),
        ),
        check_vma=False,
    )
```

```python
import functools
import math

import jax
import jax.numpy as jnp
from jax import lax
from jax.experimental import pallas as pl
from jax.experimental.pallas import tpu as pltpu
from jax.sharding import PartitionSpec as P

MESH = pl.DeviceIdType.MESH
BF = jnp.bfloat16
F32 = jnp.float32

D = 512
HEADS = 16
HD = 32
LEVELS = 13
WLAT = 6
WLON = 12
PADL = 16
TOK = 2 * WLAT * WLON
HALF = WLAT * WLON
ROWS = HALF * PADL
CHUNK = 384
GRP = 8
GW = GRP * HD
GT = GRP * TOK
EPS = 1e-05
NEG = -1e30
GRAD_GAIN = 6.0
SCALE = 1.0 / math.sqrt(HD)

NY, NX, NZ = 4, 4, 8
WIDTHS = ((512, 512), (384, 640))
PIECES = (0, 1, 2, 4, 5, 3, 6, 7, 8, 9, 12, 13, 10, 11, 14, 15)

EDGES = (0, 80, 128, 160, 240, 304)
PLACES = tuple(zip(EDGES[:-1], EDGES[1:]))
LON_AT, THREE_DIAG, TWO_DIAG, THREE_AT, TWO_AT, SIDES = EDGES
SIDES_1 = 160
FIRST = 40

(
    C_EE, C_GE, C_AW, C_XW, C_TN, C_TR, C_TC, C_TV, C_TQ0, C_TQ1, C_GN, C_AS, C_XS, C_1, C_1B, C_1LA, C_1LB, C_2, C_2B, C_2LA, C_2LB, C_3,
) = range(22)
N_COPY = 22
THREE, BOTH = 80, 144


def nt(a, b):
    return lax.dot_general(a, b, (((1,), (1,)), ((), ())), preferred_element_type=F32)


def nn(a, b):
    return lax.dot_general(a, b, (((1,), (0,)), ((), ())), preferred_element_type=F32)


def iota(shape, dim):
    return lax.broadcasted_iota(jnp.int32, shape, dim)


def split_token(t):
    level = (t >= HALF).astype(jnp.int32)
    rest = t - HALF * level
    row = lax.shift_right_logical(rest * 171, 11)
    return level, row, rest - row * WLON


def block_index(level, row, col, late_col):
    half = (col >= 6).astype(jnp.int32)
    return level * HALF + (1 - half if late_col else half) * 36 + row * 6 + col - 6 * half


def split_block(t, late_col):
    level = (t >= HALF).astype(jnp.int32)
    rest = t - HALF * level
    second = (rest >= 36).astype(jnp.int32)
    rest = rest - 36 * second
    row = lax.shift_right_logical(rest * 43, 8)
    return level, row, rest - 6 * row + 6 * (1 - second if late_col else second)


def window_index(level, row, col):
    return level * HALF + row * WLON + col


def split_part(u, rows, cols):
    size = rows * cols
    level = (u >= size).astype(jnp.int32)
    rest = u - size * level
    row = lax.shift_right_logical(rest * 171, 11) if cols == WLON else lax.shift_right_logical(rest * 43, 8)
    return level, row, rest - row * cols, u < 2 * size


def one_hot(index, keep, width):
    shape = (index.shape[0], width)
    return jnp.where(keep & (index == iota(shape, 1)), 1.0, 0.0).astype(BF)


def lon_pack(last_cols):
    level, row, col, real = split_part(iota((THREE, 1), 0), WLAT, 6)
    return one_hot(window_index(level, row, col + 6 * last_cols), real, TOK)


def block_packs(late_col):
    shapes = ((WLAT, 6, 0), (3, 6, 0), (2, 6, 4), (3, WLON, 0), (2, WLON, 4))
    first, rest = [], []
    for k, ((at, end), (rows, cols, r0)) in enumerate(zip(PLACES, shapes)):
        level, row, col, real = split_part(iota((end - at, 1), 0), rows, cols)
        if k < 3:
            first.append(one_hot(level * FIRST + (row + r0) * 6 + col, real, 2 * FIRST))
        else:
            rest.append(one_hot(block_index(level, row + r0, col, late_col), real, TOK))
    return jnp.concatenate(first, 0), jnp.concatenate(rest, 0)


def roll_matrices(row_step, col_step, last_cols):
    lv, ri, cj = split_token(iota((TOK, 1), 0))
    row, col = ri + row_step, cj + col_step
    row_in = (row >= 0) & (row < WLAT)
    col_in = (col >= 0) & (col < WLON)
    own = one_hot(block_index(lv, row, col, last_cols), row_in & col_in, TOK)
    far_col = col + (WLON // 2 if last_cols else -WLON)
    over = row >= WLAT
    far_row = jnp.where(over, row - WLAT, row + 2)
    line = far_row * WLON + col
    corner = far_row * 6 + far_col
    lon = LON_AT + lv * 36 + row * 6 + far_col
    lat = jnp.where(over, THREE_AT + lv * 36 + line, TWO_AT + lv * 24 + line)
    diag = jnp.where(over, THREE_DIAG + lv * 18 + corner, TWO_DIAG + lv * 12 + corner)
    side = jnp.where(row_in, lon, jnp.where(col_in, lat, diag))
    return own, one_hot(side, ~(row_in & col_in), SIDES)


def two_step_matrices(row_step, col_step, three_last, last_cols, place, index):
    def along_lon(level, row, col, keep):
        inside = (col >= 0) & (col < WLON)
        own = one_hot(index(level, row, col), keep & inside, TOK)
        far_col = col + (WLON // 2 if last_cols else -WLON)
        return own, one_hot(level * 36 + row * 6 + far_col, keep & (~inside), THREE)

    lv, ri, cj = place(iota((TOK, 1), 0))
    row = ri + row_step
    row_in = (row >= 0) & (row < WLAT)
    own, side = along_lon(lv, row, cj + col_step, row_in)
    over = row >= WLAT
    line = jnp.where(over, row - WLAT, row + (3 if three_last else 2)) * WLON + cj
    in_three = ~over if three_last else over
    far = one_hot(jnp.where(in_three, lv * 36 + line, THREE + lv * 24 + line), ~row_in, BOTH)
    edges = []
    for length, rows, first in ((THREE, 3, 3 if three_last else 0), (BOTH - THREE, 2, 0 if three_last else 4)):
        level, row, col, real = split_part(iota((length, 1), 0), rows, WLON)
        edges.append(along_lon(level, row + first, col + col_step, real))
    edge_own, edge_side = (jnp.concatenate([e[i] for e in edges], 0) for i in range(2))
    return own, side, far, edge_own, edge_side


def lanes_of(values, shape, dim, step):
    index = iota(shape, dim)
    out = jnp.zeros(shape, F32)
    for k, v in enumerate(values):
        out = jnp.where((index >= k * step) & (index < (k + 1) * step), v, out)
    return out


def kernel(
    late_col,
    lev_hbm, q_hbm, kvw_hbm, eo_hbm, etemp_hbm, wq_hbm, wo_hbm, stemp_hbm, lats_hbm, lons_hbm, valid_hbm, og_hbm,
    out_hbm, lg_hbm, gq_hbm, go_hbm,
    lev, kvw, eo, wq, wo, og, q_ref, etemp_ref, stemp_ref, lats_ref, lons_ref, valid_ref,
    levp, vals, prob, wexp, prod, vgrad, part, cback, rows_f, kvp, out_v, lg_v, gq_ref, go_ref,
    own_e, pk_e, rl_e,
    own_g, pk_g, rl_g, sn_g, rn_g,
    att, pk_a, rl_a, sn_a, rn_a,
    xg, pk_x, rl_x, sn_x, rn_x,
    unit, qkv, normed, rgrad, ctx, qgrad,
    m_normed, m_rgrad, m_ctx, m_qgrad,
    qs, cgs, pt, p16, bias, hmask, fold,
    early, late, s3f, s3, r3,
    lsem, ssem, rsem,
):
    lat = lax.axis_index("lat")
    lon = lax.axis_index("lon")
    y_hi = lat // 8
    x = (lat // 2) % 4
    core = lat % 2
    z = lon // 2
    y_lo = lon % 2
    y = y_hi * 2 + y_lo

    def device(yy, xx, cc, zz):
        return ((yy // 2) * 8 + xx * 2 + cc, zz * 2 + yy % 2)

    mate = (lat + 1 - 2 * core, lon)
    east = (lat, (lon + 1) % 16)
    west = (lat, (lon + 15) % 16)
    north = ((lat + 1) % 16, lon)
    south = ((lat + 15) % 16, lon)
    y_peers = [device((y + k) % NY, x, core, z) for k in range(1, NY)]
    x_peers = [device(y, (x + k) % NX, core, z) for k in range(1, NX)]
    z_peers = [device(y, x, core, (z + k) % NZ) for k in range(1, NZ)]
    lon_ahead, lon_back = (east, west) if late_col else (west, east)
    ahead = (lon_ahead, (south[0], lon_ahead[1]), (north[0], lon_ahead[1]), south, north)
    greeted = [mate, *ahead, lon_back, (north[0], lon_back[1]), (south[0], lon_back[1])] + y_peers + x_peers + z_peers
    loads = []

    def load(src, dst):
        loads.append(pltpu.make_async_copy(src, dst, lsem.at[len(loads)]))
        loads[-1].start()
        return loads[-1]

    load_og = load(og_hbm, og)
    load_kvw = load(kvw_hbm, kvw)
    load_lev = load(lev_hbm, lev)
    barrier = pltpu.get_barrier_semaphore()
    for peer in greeted:
        pl.semaphore_signal(barrier, inc=1, device_id=peer, device_id_type=MESH)
    small = [
        load(src, dst)
        for src, dst in (
            (lats_hbm, lats_ref), (lons_hbm, lons_ref), (valid_hbm, valid_ref), (q_hbm, q_ref),
            (etemp_hbm, etemp_ref), (stemp_hbm, stemp_ref),
        )
    ]

    landings = {}

    def send(src, dst, index, peer, landing=None):
        landings[index] = dst if landing is None else landing
        pltpu.make_async_remote_copy(
            src_ref=src, dst_ref=dst, send_sem=ssem.at[index], recv_sem=rsem.at[index],
            device_id=peer, device_id_type=MESH,
        ).start()

    def whole(index):
        return pltpu.make_async_remote_copy(
            src_ref=landings[index], dst_ref=landings[index], send_sem=ssem.at[index], recv_sem=rsem.at[index],
            device_id=mate, device_id_type=MESH,
        )

    def arrived(index):
        whole(index).wait_recv()

    def send_sides(places, peers):
        for (at, end), peer in zip(places, peers):
            part_of = pl.ds(at, end - at)
            send(pk_e.at[part_of], rl_e.at[part_of], C_EE, peer, rl_e)

    def send_lat(src, dst, index, three_to, two_to):
        for part_of, peer in ((pl.ds(0, THREE), three_to), (pl.ds(THREE, BOTH - THREE), two_to)):
            send(src.at[part_of], dst.at[part_of], index, peer, dst)

    pack_first, pack_rest = block_packs(late_col)
    pack_back = lon_pack(not late_col)
    tok = iota((TOK, 1), 0)
    lv, ri, cj = split_token(tok)
    own_index = functools.partial(block_index, late_col=late_col)
    own_place = functools.partial(split_block, late_col=late_col)
    olv, ori, ocj = own_place(tok)
    apart = one_hot((ori * WLON + ocj) * 2 + olv, tok >= 0, TOK)
    load_og.wait()
    for p in range(HALF):
        rows_f[2 * p : 2 * p + 2, :] = og[p].astype(F32)
    own_g[...] = nn(apart, rows_f[...].astype(BF)).astype(BF)
    glv, gri, gcj, greal = split_part(iota((THREE, 1), 0), WLAT, 6)
    pk_g[...] = nn(one_hot(glv * HALF + gri * 6 + gcj, greal, TOK), own_g[...]).astype(BF)
    pl.semaphore_wait(barrier, len(greeted))
    send(pk_g, rl_g, C_GE, lon_ahead)
    for copy in small:
        copy.wait()
    s = lats_ref[0]
    t = lons_ref[0]
    late_row = s > WLAT // 2
    row_step = jnp.where(late_row, s - WLAT, s)
    col_step = t - WLON if late_col else t
    sel_own, sel_side = roll_matrices(row_step, col_step, late_col)
    kvp[...] = jnp.zeros((8, D), F32)
    kvp[0:WLAT, 0:WLON] = valid_ref[...].astype(F32)

    def with_valid(sides, places):
        pieces, base = [], places[0][0]
        for at, end in places:
            pieces += [sides[at - base : end - base - 8], kvp[...]]
        return jnp.concatenate(pieces, 0).astype(BF)

    q_rows = jnp.concatenate([jnp.broadcast_to(q_ref[l : l + 1, :], (HEADS, D)) for l in range(2)], 0)
    row_head = iota((2 * HEADS, D), 0) % HEADS
    lane_head = lax.shift_right_logical(iota((2 * HEADS, D), 1), 5)
    q_rows = jnp.where(row_head == lane_head, q_rows.astype(F32), 0.0).astype(BF)
    lane_scale = lanes_of([etemp_ref[h] * SCALE for h in range(HEADS)] * 2, (1, 2 * HEADS), 1, 1)
    load_kvw.wait()
    load_lev.wait()
    load_eo = load(eo_hbm, eo)
    load_wo = load(wo_hbm, wo)
    wq_sem = lsem.at[len(loads)]
    for src, dst, width in ((0, 0, GW), (D, GW, GW), (GW, D, GW), (D + GW, D + GW, GW), (2 * D, 2 * D, D)):
        pltpu.make_async_copy(wq_hbm.at[:, pl.ds(src, width)], wq.at[:, pl.ds(dst, width)], wq_sem).start()
    filler = jnp.zeros((6, PADL - LEVELS, D), BF)

    def run_of(k):
        return 12 * (k % WLAT) + 6 * ((k // WLAT) ^ int(late_col))

    for k in range(2 * WLAT):
        block = jnp.concatenate([lev[run_of(k) : run_of(k) + 6], filler], 1)
        levp[6 * PADL * k : 6 * PADL * (k + 1), :] = block.reshape(6 * PADL, D)
    spread_row = iota((2 * HEADS, 2 * D), 0)
    spread = jnp.where(lax.shift_right_logical(iota((2 * HEADS, 2 * D), 1), 5) == spread_row, 1.0, 0.0).astype(BF)

    def encode_rows(low, high):
        rows, count = slice(low, high), (high - low) // PADL
        kv = nn(levp[rows, :], kvw[...])
        vals[rows, :] = kv[:, D:].astype(BF)
        sc = (nt(kv[:, :D].astype(BF), q_rows) * lane_scale).reshape(count, PADL, 2 * HEADS)
        sc = jnp.where(iota((count, PADL, 2 * HEADS), 1) < LEVELS, sc, NEG)
        e = jnp.exp(sc - jnp.max(sc, 1, keepdims=True))
        pm = e * (1.0 / jnp.sum(e, 1, keepdims=True))
        prob[rows, :] = pm.reshape(high - low, 2 * HEADS)

    def context_of(c):
        rows = slice(8 * PADL * c, 8 * PADL * (c + 1))
        w = nn(prob[rows, :].astype(BF), spread)
        wexp[rows, :] = w.astype(BF)
        v = vals[rows, :].astype(F32)
        for l in range(2):
            product = (w[:, l * D : (l + 1) * D] * v).reshape(8, 2, 8, D)
            product = (product[:, 0] + product[:, 1]).reshape(64, D)
            for j in range(4):
                part[4 * l + j, 64 * c : 64 * (c + 1), :] = product[:, 128 * j : 128 * (j + 1)]
        for l in range(2):
            for j in range(4):
                acc = part[4 * l + j, pl.ds(64 * c, 8, stride=8), :]
                for m in range(1, 8):
                    acc = acc + part[4 * l + j, pl.ds(64 * c + m, 8, stride=8), :]
                cback[l * HALF + 8 * c : l * HALF + 8 * (c + 1), 128 * j : 128 * (j + 1)] = acc

    def encoded_of(low, high):
        count = high - low
        context = jnp.concatenate([cback[low:high, :], cback[HALF + low : HALF + high, :]], 0)
        mixed = nn(context.astype(BF), eo[...])
        second = iota((2 * count, D), 0) >= count
        query = jnp.where(second, q_ref[1:2, :].astype(F32), q_ref[0:1, :].astype(F32))
        result = (query + mixed).astype(BF)
        for l in range(2):
            rows_f[l * HALF + low : l * HALF + high, :] = result[l * count : (l + 1) * count].astype(F32)
        return result

    encode_rows(0, 320)
    encode_rows(320, 640)
    for c in range(FIRST // 8):
        context_of(c)
    load_eo.wait()
    pk_e[:SIDES_1, :] = with_valid(nn(pack_first, encoded_of(0, FIRST)), PLACES[:3])
    send_sides(PLACES[:3], ahead[:3])
    encode_rows(640, 896)
    encode_rows(896, 1152)
    for c in range(FIRST // 8, HALF // 8):
        context_of(c)
    encoded_of(FIRST, HALF)
    own_e[...] = rows_f[...].astype(BF)
    pk_e[SIDES_1:, :] = with_valid(nn(pack_rest, own_e[...]), PLACES[3:])
    send_sides(PLACES[3:], ahead[3:])
    near = nn(sel_own, own_e[...])
    two_own, two_side, two_far, two_edge_own, two_edge_side = two_step_matrices(
        row_step, col_step, False, late_col, split_token, own_index
    )
    near_g = nn(two_own, own_g[...])
    edge_g = nn(two_edge_own, own_g[...])
    tq = iota((1, GT), 1)
    for k in range(1, GRP):
        tq = jnp.where(iota((1, GT), 1) >= k * TOK, iota((1, GT), 1) - k * TOK, tq)
    qri = split_token(tq)[1]
    first_wrapped = 16 * WLAT - s
    window_row = jnp.where(late_row, (lat + 15) % 16, lat) * WLAT
    wk = jnp.where(window_row + ri >= first_wrapped, 1, 0)
    wqv = jnp.where(window_row + qri >= first_wrapped, 1, 0)
    kk = iota((TOK, GT), 0)
    fold[...] = jnp.where(kk == tq, 1.0, 0.0).astype(BF)
    fh = lax.shift_right_logical(iota((GW, GT), 0), 5)
    lane_t = iota((GW, GT), 1)
    hmask[...] = jnp.where((lane_t >= fh * TOK) & (lane_t < (fh + 1) * TOK), 1.0, 0.0).astype(BF)
    group_head = lax.shift_right_logical(iota((TOK, GW), 1), 5)
    eye = jnp.where(iota((GW, GW), 0) == iota((GW, GW), 1), 1.0, 0.0).astype(BF)
    scale_rows = [
        lanes_of([stemp_ref[g * GRP + h] * SCALE for h in range(GRP)], (1, GT), 1, TOK) for g in range(2)
    ]
    n = iota((256, 1), 0)
    bit = lambda shift, mask: lax.shift_right_logical(n, shift) & mask
    wrow = bit(7, 1) * 256 + bit(4, 3) * 64 + core * 32 + bit(1, 7) * 4 + bit(6, 1) * 2 + (n & 1)
    pick = one_hot(wrow, n >= 0, D)

    back_own, back_side, back_far, bedge_own, bedge_side = two_step_matrices(
        -row_step, -col_step, True, not late_col, own_place, window_index
    )
    pltpu.make_async_copy(wq_hbm, wq, wq_sem).wait()
    arrived(C_GE)
    sn_g[...] = (edge_g + nn(two_edge_side, rl_g[...])).astype(BF)
    send_lat(sn_g, rn_g, C_GN, south, north)
    near_g = near_g + nn(two_side, rl_g[...])
    arrived(C_EE)
    beside = rl_e[THREE_DIAG - 8 : THREE_DIAG, :].astype(F32) if late_col else kvp[...]
    end = THREE_AT if late_col else SIDES
    valid_2 = jnp.where(late_row, rl_e[end - 8 : end, :].astype(F32), beside)
    lane = iota((TOK, 128), 1)
    valid_row = jnp.zeros((TOK, 128), F32)
    for r in range(WLAT):
        valid_row = jnp.where(ri == r, valid_2[r : r + 1, :128], valid_row)
    valid_k = jnp.sum(jnp.where(lane == cj, valid_row, 0.0), 1, keepdims=True)
    ok = (wk == wqv) & ((valid_k > 0.5) | (kk == tq))
    bias[...] = jnp.where(ok, 0.0, NEG)
    rolled = near + nn(sel_side, rl_e[...])

    mean = jnp.mean(rolled, 1, keepdims=True)
    centered = rolled - mean
    inv = lax.rsqrt(jnp.mean(centered * centered, 1, keepdims=True) + EPS)
    unit_v = centered * inv
    unit[...] = unit_v
    normed[...] = unit_v.astype(BF)
    send(normed, m_normed, C_TN, mate)
    qkv[...] = nn(normed[...], wq[...]).astype(BF)
    scores, values_t, turned = [], [], []
    for g in range(2):
        qg = qkv[:, g * D : g * D + GW]
        for h in range(GRP):
            qs[g, h * TOK : (h + 1) * TOK, :] = jnp.where(group_head == h, qg, jnp.zeros_like(qg))
        scores.append(nt(qkv[:, g * D + GW : (g + 1) * D], qs[g]))
    for g in range(2):
        values_t.append(nt(eye, qkv[:, 2 * D + g * GW : 2 * D + (g + 1) * GW]).astype(BF))
    for g in range(2):
        st = scores[g] * scale_rows[g] + bias[...]
        e = jnp.exp(st - jnp.max(st, 0, keepdims=True))
        p = e * (1.0 / jnp.sum(e, 0, keepdims=True))
        pt[g] = p
        p16[g] = p.astype(BF)
        turned.append(nn(values_t[g], p16[g]).astype(BF) * hmask[...])
    for g in range(2):
        ctx[:, g * GW : (g + 1) * GW] = nt(fold[...], turned[g]).astype(BF)
    send(ctx, m_ctx, C_TC, mate)
    load_wo.wait()
    att[...] = nn(ctx[...], wo[...]).astype(BF)
    pk_a[...] = nn(pack_back, att[...]).astype(BF)
    send(pk_a, rl_a, C_AW, lon_back)
    arrived(C_GN)
    rgrad[...] = (near_g + nn(two_far, rn_g[...])).astype(BF)
    send(rgrad, m_rgrad, C_TR, mate)
    cgrad = nt(rgrad[...], wo[...]).astype(BF)
    for g in range(2):
        piece = cgrad[:, g * GW : (g + 1) * GW]
        for h in range(GRP):
            cgs[g, h * TOK : (h + 1) * TOK, :] = jnp.where(group_head == h, piece, jnp.zeros_like(piece))
    for g in range(2):
        qgrad[:, 2 * D + g * GW : 2 * D + (g + 1) * GW] = nn(p16[g], cgs[g]).astype(BF)
    third = [pl.ds(k * D, D) for k in range(3)]
    send(qgrad.at[:, third[2]], m_qgrad.at[:, third[2]], C_TV, mate)

    def scores_back(g):
        p = pt[g]
        dp = nt(qkv[:, 2 * D + g * GW : 2 * D + (g + 1) * GW], cgs[g])
        ds = p * (dp - jnp.sum(p * dp, 0, keepdims=True)) * scale_rows[g]
        ds16 = ds.astype(BF)
        k_t = nt(eye, qkv[:, g * D + GW : (g + 1) * D]).astype(BF)
        q_t = nn(k_t, ds16).astype(BF) * hmask[...]
        qgrad[:, g * D : g * D + GW] = nt(fold[...], q_t).astype(BF)
        qgrad[:, g * D + GW : (g + 1) * D] = nn(ds16, qs[g]).astype(BF)
        send(qgrad.at[:, third[g]], m_qgrad.at[:, third[g]], C_TQ0 + g, mate)

    def picked(left, m_left):
        return nt(pick, left[...]).astype(BF), nt(pick, m_left[...]).astype(BF)

    def chip_sum(lefts, right, m_right):
        total = nn(lefts[0], right) + nn(lefts[1], m_right)
        return total.astype(BF).reshape(NY, NX, 16, right.shape[1])

    def share(k_set, low_a, width_a, low_b, width_b):
        send_a, send_b, r1a, r1b = (early, late)[k_set][:4]
        a, b = pl.ds(low_a, width_a), pl.ds(low_b, width_b)
        for k in range(1, NY):
            src = send_a.at[(y + k) % NY, :, :, a]
            send(src, r1a.at[k - 1, :, :, a], C_1 + 2 * k_set, y_peers[k - 1], r1a)
        for k in range(1, NX):
            src = send_b.at[:, (x + k) % NX, :, b]
            send(src, r1b.at[k - 1, :, :, b], C_1 + 2 * k_set + 1, x_peers[k - 1], r1b)

    def second_stage(k_set):
        send_a, send_b, r1a, r1b, s2a, s2b, r2a, r2b = (early, late)[k_set]
        arrived(C_1 + 2 * k_set)
        arrived(C_1 + 2 * k_set + 1)
        sum_a = send_a[y].astype(F32)
        sum_b = send_b[:, x].astype(F32)
        for k in range(3):
            sum_a = sum_a + r1a[k].astype(F32)
            sum_b = sum_b + r1b[k].astype(F32)
        s2a[...] = sum_a.astype(BF)
        s2b[...] = sum_b.astype(BF)
        for k in range(1, NX):
            send(s2a.at[(x + k) % NX], r2a.at[k - 1], C_2 + 2 * k_set, x_peers[k - 1], r2a)
        for k in range(1, NY):
            send(s2b.at[(y + k) % NY], r2b.at[k - 1], C_2 + 2 * k_set + 1, y_peers[k - 1], r2b)

    def second_sums(k_set):
        s2a, s2b, r2a, r2b = (early, late)[k_set][4:]
        arrived(C_2 + 2 * k_set)
        arrived(C_2 + 2 * k_set + 1)
        sum_a = s2a[x].astype(F32)
        sum_b = s2b[y].astype(F32)
        for k in range(3):
            sum_a = sum_a + r2a[k].astype(F32)
            sum_b = sum_b + r2b[k].astype(F32)
        return sum_a, sum_b

    scores_back(0)
    arrived(C_TC)
    arrived(C_TR)
    g_out = chip_sum(picked(ctx, m_ctx), rgrad[...], m_rgrad[...])
    early[0][:, :, :, 256:] = g_out[:, :, :, :256]
    early[1][:, :, :, 256:] = g_out[:, :, :, 256:]
    share(0, 256, 256, 256, 256)
    arrived(C_TN)
    arrived(C_TV)
    lefts = picked(normed, m_normed)
    g_val = chip_sum(lefts, qgrad[:, 2 * D :], m_qgrad[:, 2 * D :])
    early[0][:, :, :, :256] = g_val[:, :, :, :256]
    early[1][:, :, :, :256] = g_val[:, :, :, 256:]
    share(0, 0, 256, 0, 256)
    scores_back(1)

    def sum_qk(g):
        arrived(C_TQ0 + g)
        return chip_sum(lefts, qgrad[:, g * D : (g + 1) * D], m_qgrad[:, g * D : (g + 1) * D])

    g_qk = sum_qk(0)
    late[0][:, :, :, :256] = g_qk[:, :, :, :256]
    late[1][:, :, :, :256] = g_qk[:, :, :, 256:]
    share(1, 0, 256, 0, 256)
    ugrad = nt(qgrad[...], wq[...])
    u = unit[...]
    xgrad = inv * (
        ugrad - jnp.mean(ugrad, 1, keepdims=True) - u * jnp.mean(ugrad * u, 1, keepdims=True)
    )
    xg[...] = xgrad.astype(BF)
    pk_x[...] = nn(pack_back, xg[...]).astype(BF)
    send(pk_x, rl_x, C_XW, lon_back)
    g_qk = sum_qk(1)
    late[0][:, :, :, 256:] = g_qk[:, :, :, :128]
    late[1][:, :, :, 256:] = g_qk[:, :, :, 128:]
    share(1, 256, 128, 256, 384)
    near_x = own_g[...].astype(F32) + nn(back_own, xg[...])
    key_q = nt(q_rows, kvw[:, :D]).astype(BF)
    edge_x = nn(bedge_own, xg[...])
    second_stage(0)
    arrived(C_XW)
    sn_x[...] = (edge_x + nn(bedge_side, rl_x[...])).astype(BF)
    send_lat(sn_x, rn_x, C_XS, north, south)
    near_x = near_x + nn(back_side, rl_x[...])
    second_stage(1)
    arrived(C_XS)
    arrived(C_AW)
    sn_a[...] = (nn(bedge_own, att[...]) + nn(bedge_side, rl_a[...])).astype(BF)
    send_lat(sn_a, rn_a, C_AS, north, south)
    egrad = (near_x + nn(back_far, rn_x[...])).astype(BF)

    cback[...] = nt(egrad, eo[...]).astype(BF).astype(F32)

    def products(c, carry):
        first = cback[pl.ds(pl.multiple_of(8 * c, 8), 8), :]
        second = cback[pl.ds(pl.multiple_of(HALF + 8 * c, 8), 8), :]
        for p in range(8):
            rows = pl.ds(pl.multiple_of(8 * PADL * c + p * PADL, PADL), PADL)
            c0, c1 = first[p : p + 1, :], second[p : p + 1, :]
            v = vals[rows, :].astype(F32)
            prod[rows, :D] = (c0 * v).astype(BF)
            prod[rows, D:] = (c1 * v).astype(BF)
            vgrad[rows, :] = (wexp[rows, :D].astype(F32) * c0 + wexp[rows, D:].astype(F32) * c1).astype(BF)
        return carry

    lax.fori_loop(0, HALF // 8, products, 0)

    sums = [*second_sums(1), *second_sums(0)]
    chunks = [v[:, 128 * i : 128 * (i + 1)] for v in sums for i in range(v.shape[1] // 128)]
    for i, value in enumerate(chunks):
        s3f[i % 2, pl.ds(i // 2, 16, stride=8), :] = value
    for k in range(NZ):
        for h in range(2):
            s3[k, :, 128 * h : 128 * (h + 1)] = s3f[h, 16 * k : 16 * (k + 1), :].astype(BF)
    for k in range(1, NZ):
        send(s3.at[(z + k) % NZ], r3.at[k - 1], C_3, z_peers[k - 1], r3)

    for c in range(ROWS // CHUNK):
        rows = slice(c * CHUNK, (c + 1) * CHUNK)
        pg = nt(prod[rows, :], spread).reshape(CHUNK // PADL, PADL, 2 * HEADS)
        pm = prob[rows, :].reshape(CHUNK // PADL, PADL, 2 * HEADS)
        sg = pm * (pg - jnp.sum(pm * pg, 1, keepdims=True))
        prob[rows, :] = sg.reshape(CHUNK, 2 * HEADS) * lane_scale

    def level_grads(c):
        rows = slice(c * CHUNK, (c + 1) * CHUNK)
        lg = nt(vgrad[rows, :], kvw[:, D:]) + nn(prob[rows, :].astype(BF), key_q)
        lg = lg.astype(BF).reshape(CHUNK // PADL, PADL, D)
        for k in range(4):
            lg_v[run_of(4 * c + k) : run_of(4 * c + k) + 6] = lg[6 * k : 6 * (k + 1), :LEVELS, :]

    for c in range(3):
        level_grads(c)
    stores = [pltpu.make_async_copy(lg_v, lg_hbm, lsem.at[len(loads) + 1])]
    stores[-1].start()
    arrived(C_AS)
    added = nn(back_own, att[...]) + nn(back_side, rl_a[...]) + nn(back_far, rn_a[...])
    out16 = (own_e[...].astype(F32) + added).astype(BF)
    u_row = iota((TOK, 1), 0)
    u_patch = lax.shift_right_logical(u_row, 1)
    u_lat = lax.shift_right_logical(u_patch * 171, 11)
    together = one_hot(own_index(u_row & 1, u_lat, u_patch - u_lat * WLON), u_row >= 0, TOK)
    rows_f[...] = nn(together, out16)
    for p in range(HALF):
        out_v[p] = rows_f[2 * p : 2 * p + 2, :].astype(BF)
    stores.append(pltpu.make_async_copy(out_v, out_hbm, lsem.at[len(loads) + 2]))
    stores[-1].start()

    arrived(C_3)
    factor = GRAD_GAIN * (2 * 96 * 192) ** (-0.5)
    for h in range(2):
        total = s3f[h, pl.ds(pl.multiple_of(16 * z, 16), 16), :]
        for k in range(NZ - 1):
            total = total + r3[k, :, 128 * h : 128 * (h + 1)].astype(F32)
        total = total * factor
        for b in range(2):
            for j in range(8):
                piece = total[8 * b + j : 8 * b + j + 1, :]
                place = PIECES[2 * j + h]
                if place < 12:
                    gq_ref[12 * b + place : 12 * b + place + 1, :] = piece
                else:
                    go_ref[4 * b + place - 12 : 4 * b + place - 11, :] = piece
    for i, (src, dst) in enumerate(((gq_ref, gq_hbm), (go_ref, go_hbm))):
        stores.append(pltpu.make_async_copy(src, dst, lsem.at[len(loads) + 3 + i]))
        stores[-1].start()
    for index in landings:
        whole(index).wait_send()
    for copy in stores:
        copy.wait()


def deliver(a, b, c, d, a_out, b_out, c_out, d_out, sems):
    pairs = ((a, a_out), (b, b_out), (c, c_out), (d, d_out))
    copies = [pltpu.make_async_copy(src, dst, sems.at[i]) for i, (src, dst) in enumerate(pairs)]
    for copy in copies:
        copy.start()
    for copy in copies:
        copy.wait()


def local(levels_in, latent_queries, enc_kv, enc_out, enc_temp, w_qkv, w_out, swin_temp, lat_shift, lon_shift, key_valid, output_grad):
    hbm = pl.BlockSpec(memory_space=pl.ANY)
    V = pltpu.VMEM
    block = lambda rows: V((rows, D), BF)
    scratch = [
        V((HALF, LEVELS, D), BF), V((D, 2 * D), BF), V((D, D), BF), V((D, 3 * D), BF), V((D, D), BF), V((HALF, 2, D), BF),
        V((2, D), BF), pltpu.SMEM((HEADS,), F32), pltpu.SMEM((HEADS,), F32), pltpu.SMEM((1,), jnp.int32),
        pltpu.SMEM((1,), jnp.int32), V((WLAT, WLON), jnp.int32),
        V((ROWS, D), BF),
        V((ROWS, D), BF),
        V((ROWS, 2 * HEADS), F32),
        V((ROWS, 2 * D), BF),
        V((ROWS, 2 * D), BF),
        V((ROWS, D), BF),
        V((8, 8 * HALF, 128), F32),
        V((TOK, D), F32),
        V((TOK, D), F32),
        V((8, D), F32),
        V((HALF, 2, D), BF),
        V((HALF, LEVELS, D), BF),
        V((24, 128), F32), V((8, 128), F32),
    ]
    scratch += [block(TOK), block(SIDES), block(SIDES)]
    for _ in range(3):
        scratch += [block(TOK), block(THREE), block(THREE), block(BOTH), block(BOTH)]
    scratch += [
        V((TOK, D), F32), V((TOK, 3 * D), BF), block(TOK), block(TOK), block(TOK), V((TOK, 3 * D), BF),
        block(TOK), block(TOK), block(TOK), V((TOK, 3 * D), BF),
        V((2, GT, GW), BF), V((2, GT, GW), BF), V((2, TOK, GT), F32), V((2, TOK, GT), BF),
        V((TOK, GT), F32), V((GW, GT), BF), V((TOK, GT), BF),
        *(
            tuple(V((*lead, 16, w), BF) for lead in ((NY, NX), (3, NX), (NX,), (3,)) for w in pair)
            for pair in WIDTHS
        ),
        V((2, 128, 128), F32), V((NZ, 16, 256), BF), V((NZ - 1, 16, 256), BF),
        pltpu.SemaphoreType.DMA((16,)),
        pltpu.SemaphoreType.DMA((N_COPY,)),
        pltpu.SemaphoreType.DMA((N_COPY,)),
    ]
    lev = jnp.transpose(levels_in, (1, 2, 0, 3)).reshape(HALF, LEVELS, D)
    og = jnp.transpose(output_grad, (1, 2, 0, 3)).reshape(HALF, 2, D)
    shapes = (
        jax.ShapeDtypeStruct((HALF, 2, D), BF),
        jax.ShapeDtypeStruct((HALF, LEVELS, D), BF),
        jax.ShapeDtypeStruct((24, 128), F32),
        jax.ShapeDtypeStruct((8, 128), F32),
    )

    def run(late_col):
        return pl.pallas_call(
            functools.partial(kernel, late_col),
            out_shape=shapes,
            in_specs=[hbm] * 12,
            out_specs=(hbm,) * 4,
            scratch_shapes=scratch,
            compiler_params=pltpu.CompilerParams(
                collective_id=int(late_col), has_side_effects=True, vmem_limit_bytes=48 * 1024 * 1024
            ),
        )

    parts = lax.cond(
        lon_shift[0] > WLON // 2, run(True), run(False),
        lev, latent_queries, enc_kv, enc_out, enc_temp, w_qkv, w_out, swin_temp, lat_shift, lon_shift, key_valid, og,
    )
    out, lg, gq, go = pl.pallas_call(
        deliver,
        out_shape=shapes,
        in_specs=[hbm] * 4,
        out_specs=(hbm,) * 4,
        scratch_shapes=[pltpu.SemaphoreType.DMA((4,))],
    )(*parts)
    out = jnp.transpose(out.reshape(WLAT, WLON, 2, D), (2, 0, 1, 3))
    lg = jnp.transpose(lg.reshape(WLAT, WLON, LEVELS, D), (2, 0, 1, 3))
    return out, lg, gq.reshape(-1), go.reshape(-1)


def solution(mesh):
    return jax.shard_map(
        local,
        mesh=mesh,
        in_specs=(
            P(None, "lat", "lon", None), P(), P(), P(), P(), P(), P(), P(), P(), P(),
            P("lat", "lon"),
            P(None, "lat", "lon", None),
        ),
        out_specs=(
            P(None, "lat", "lon", None),
            P(None, "lat", "lon", None),
            P(("lat", "lon")),
            P(("lat", "lon")),
        ),
        check_vma=False,
    )
```

```python
import functools
import math

import jax
import jax.numpy as jnp
from jax import lax
from jax.experimental import pallas as pl
from jax.experimental.pallas import tpu as pltpu
from jax.sharding import PartitionSpec as P

MESH = pl.DeviceIdType.MESH
BF = jnp.bfloat16
F32 = jnp.float32

D = 512
HEADS = 16
HD = 32
LEVELS = 13
WLAT = 6
WLON = 12
PADL = 16
TOK = 2 * WLAT * WLON
HALF = WLAT * WLON
ROWS = HALF * PADL
CHUNK = 384
GRP = 8
GW = GRP * HD
GT = GRP * TOK
EPS = 1e-05
NEG = -1e30
GRAD_GAIN = 6.0
SCALE = 1.0 / math.sqrt(HD)

NY, NX, NZ = 4, 4, 8
WIDTHS = ((512, 512), (384, 640))
PIECES = (0, 1, 2, 4, 5, 3, 6, 7, 8, 9, 12, 13, 10, 11, 14, 15)

EDGES = (0, 80, 128, 160, 240, 304)
PLACES = tuple(zip(EDGES[:-1], EDGES[1:]))
LON_AT, THREE_DIAG, TWO_DIAG, THREE_AT, TWO_AT, SIDES = EDGES
SIDES_1 = 160
FIRST = 40

(
    C_EE, C_GE, C_AW, C_XW, C_TN, C_TR, C_TC, C_TV, C_TQ0, C_TQ1, C_GN, C_AS, C_XS, C_1, C_1B, C_1LA, C_1LB, C_2, C_2B, C_2LA, C_2LB, C_3,
) = range(22)
N_COPY = 22
THREE, BOTH = 80, 144


def nt(a, b):
    return lax.dot_general(a, b, (((1,), (1,)), ((), ())), preferred_element_type=F32)


def nn(a, b):
    return lax.dot_general(a, b, (((1,), (0,)), ((), ())), preferred_element_type=F32)


def iota(shape, dim):
    return lax.broadcasted_iota(jnp.int32, shape, dim)


def split_token(t):
    level = (t >= HALF).astype(jnp.int32)
    rest = t - HALF * level
    row = lax.shift_right_logical(rest * 171, 11)
    return level, row, rest - row * WLON


def block_index(level, row, col, late_col):
    half = (col >= 6).astype(jnp.int32)
    return level * HALF + (1 - half if late_col else half) * 36 + row * 6 + col - 6 * half


def split_block(t, late_col):
    level = (t >= HALF).astype(jnp.int32)
    rest = t - HALF * level
    second = (rest >= 36).astype(jnp.int32)
    rest = rest - 36 * second
    row = lax.shift_right_logical(rest * 43, 8)
    return level, row, rest - 6 * row + 6 * (1 - second if late_col else second)


def window_index(level, row, col):
    return level * HALF + row * WLON + col


def split_part(u, rows, cols):
    size = rows * cols
    level = (u >= size).astype(jnp.int32)
    rest = u - size * level
    row = lax.shift_right_logical(rest * 171, 11) if cols == WLON else lax.shift_right_logical(rest * 43, 8)
    return level, row, rest - row * cols, u < 2 * size


def one_hot(index, keep, width):
    shape = (index.shape[0], width)
    return jnp.where(keep & (index == iota(shape, 1)), 1.0, 0.0).astype(BF)


def lon_pack(last_cols):
    level, row, col, real = split_part(iota((THREE, 1), 0), WLAT, 6)
    return one_hot(window_index(level, row, col + 6 * last_cols), real, TOK)


def block_packs(late_col):
    shapes = ((WLAT, 6, 0), (3, 6, 0), (2, 6, 4), (3, WLON, 0), (2, WLON, 4))
    first, rest = [], []
    for k, ((at, end), (rows, cols, r0)) in enumerate(zip(PLACES, shapes)):
        level, row, col, real = split_part(iota((end - at, 1), 0), rows, cols)
        if k < 3:
            first.append(one_hot(level * FIRST + (row + r0) * 6 + col, real, 2 * FIRST))
        else:
            rest.append(one_hot(block_index(level, row + r0, col, late_col), real, TOK))
    return jnp.concatenate(first, 0), jnp.concatenate(rest, 0)


def roll_matrices(row_step, col_step, last_cols):
    lv, ri, cj = split_token(iota((TOK, 1), 0))
    row, col = ri + row_step, cj + col_step
    row_in = (row >= 0) & (row < WLAT)
    col_in = (col >= 0) & (col < WLON)
    own = one_hot(block_index(lv, row, col, last_cols), row_in & col_in, TOK)
    far_col = col + (WLON // 2 if last_cols else -WLON)
    over = row >= WLAT
    far_row = jnp.where(over, row - WLAT, row + 2)
    line = far_row * WLON + col
    corner = far_row * 6 + far_col
    lon = LON_AT + lv * 36 + row * 6 + far_col
    lat = jnp.where(over, THREE_AT + lv * 36 + line, TWO_AT + lv * 24 + line)
    diag = jnp.where(over, THREE_DIAG + lv * 18 + corner, TWO_DIAG + lv * 12 + corner)
    side = jnp.where(row_in, lon, jnp.where(col_in, lat, diag))
    return own, one_hot(side, ~(row_in & col_in), SIDES)


def two_step_matrices(row_step, col_step, three_last, last_cols, place, index):
    def along_lon(level, row, col, keep):
        inside = (col >= 0) & (col < WLON)
        own = one_hot(index(level, row, col), keep & inside, TOK)
        far_col = col + (WLON // 2 if last_cols else -WLON)
        return own, one_hot(level * 36 + row * 6 + far_col, keep & (~inside), THREE)

    lv, ri, cj = place(iota((TOK, 1), 0))
    row = ri + row_step
    row_in = (row >= 0) & (row < WLAT)
    own, side = along_lon(lv, row, cj + col_step, row_in)
    over = row >= WLAT
    line = jnp.where(over, row - WLAT, row + (3 if three_last else 2)) * WLON + cj
    in_three = ~over if three_last else over
    far = one_hot(jnp.where(in_three, lv * 36 + line, THREE + lv * 24 + line), ~row_in, BOTH)
    edges = []
    for length, rows, first in ((THREE, 3, 3 if three_last else 0), (BOTH - THREE, 2, 0 if three_last else 4)):
        level, row, col, real = split_part(iota((length, 1), 0), rows, WLON)
        edges.append(along_lon(level, row + first, col + col_step, real))
    edge_own, edge_side = (jnp.concatenate([e[i] for e in edges], 0) for i in range(2))
    return own, side, far, edge_own, edge_side


def lanes_of(values, shape, dim, step):
    index = iota(shape, dim)
    out = jnp.zeros(shape, F32)
    for k, v in enumerate(values):
        out = jnp.where((index >= k * step) & (index < (k + 1) * step), v, out)
    return out


def kernel(
    late_col,
    lev_hbm, q_hbm, kvw_hbm, eo_hbm, etemp_hbm, wq_hbm, wo_hbm, stemp_hbm, lats_hbm, lons_hbm, valid_hbm, og_hbm,
    out_hbm, lg_hbm, gq_hbm, go_hbm,
    lev, kvw, eo, wq, wo, og, q_ref, etemp_ref, stemp_ref, lats_ref, lons_ref, valid_ref,
    levp, vals, prob, wexp, prod, vgrad, part, cback, rows_f, kvp, out_v, lg_v, gq_ref, go_ref,
    own_e, pk_e, rl_e,
    own_g, pk_g, rl_g, sn_g, rn_g,
    att, pk_a, rl_a, sn_a, rn_a,
    xg, pk_x, rl_x, sn_x, rn_x,
    unit, qkv, normed, rgrad, ctx, qgrad,
    m_normed, m_rgrad, m_ctx, m_qgrad,
    qs, cgs, pt, p16, bias, hmask, fold,
    early, late, s3f, s3, r3,
    lsem, ssem, rsem,
):
    lat = lax.axis_index("lat")
    lon = lax.axis_index("lon")
    y_hi = lat // 8
    x = (lat // 2) % 4
    core = lat % 2
    z = lon // 2
    y_lo = lon % 2
    y = y_hi * 2 + y_lo

    def device(yy, xx, cc, zz):
        return ((yy // 2) * 8 + xx * 2 + cc, zz * 2 + yy % 2)

    mate = (lat + 1 - 2 * core, lon)
    east = (lat, (lon + 1) % 16)
    west = (lat, (lon + 15) % 16)
    north = ((lat + 1) % 16, lon)
    south = ((lat + 15) % 16, lon)
    y_peers = [device((y + k) % NY, x, core, z) for k in range(1, NY)]
    x_peers = [device(y, (x + k) % NX, core, z) for k in range(1, NX)]
    z_peers = [device(y, x, core, (z + k) % NZ) for k in range(1, NZ)]
    lon_ahead, lon_back = (east, west) if late_col else (west, east)
    ahead = (lon_ahead, (south[0], lon_ahead[1]), (north[0], lon_ahead[1]), south, north)
    greeted = [mate, *ahead, lon_back, (north[0], lon_back[1]), (south[0], lon_back[1])] + y_peers + x_peers + z_peers
    loads = []

    def load(src, dst):
        loads.append(pltpu.make_async_copy(src, dst, lsem.at[len(loads)]))
        loads[-1].start()
        return loads[-1]

    load_og = load(og_hbm, og)
    load_kvw = load(kvw_hbm, kvw)
    load_lev = load(lev_hbm, lev)
    barrier = pltpu.get_barrier_semaphore()
    for peer in greeted:
        pl.semaphore_signal(barrier, inc=1, device_id=peer, device_id_type=MESH)
    small = [
        load(src, dst)
        for src, dst in (
            (lats_hbm, lats_ref), (lons_hbm, lons_ref), (valid_hbm, valid_ref), (q_hbm, q_ref),
            (etemp_hbm, etemp_ref), (stemp_hbm, stemp_ref),
        )
    ]

    landings = {}

    def send(src, dst, index, peer, landing=None):
        landings[index] = dst if landing is None else landing
        pltpu.make_async_remote_copy(
            src_ref=src, dst_ref=dst, send_sem=ssem.at[index], recv_sem=rsem.at[index],
            device_id=peer, device_id_type=MESH,
        ).start()

    def whole(index):
        return pltpu.make_async_remote_copy(
            src_ref=landings[index], dst_ref=landings[index], send_sem=ssem.at[index], recv_sem=rsem.at[index],
            device_id=mate, device_id_type=MESH,
        )

    def arrived(index):
        whole(index).wait_recv()

    def send_sides(places, peers):
        for (at, end), peer in zip(places, peers):
            part_of = pl.ds(at, end - at)
            send(pk_e.at[part_of], rl_e.at[part_of], C_EE, peer, rl_e)

    def send_lat(src, dst, index, three_to, two_to):
        for part_of, peer in ((pl.ds(0, THREE), three_to), (pl.ds(THREE, BOTH - THREE), two_to)):
            send(src.at[part_of], dst.at[part_of], index, peer, dst)

    pack_first, pack_rest = block_packs(late_col)
    pack_back = lon_pack(not late_col)
    tok = iota((TOK, 1), 0)
    lv, ri, cj = split_token(tok)
    own_index = functools.partial(block_index, late_col=late_col)
    own_place = functools.partial(split_block, late_col=late_col)
    olv, ori, ocj = own_place(tok)
    apart = one_hot((ori * WLON + ocj) * 2 + olv, tok >= 0, TOK)
    load_og.wait()
    for p in range(HALF):
        rows_f[2 * p : 2 * p + 2, :] = og[p].astype(F32)
    own_g[...] = nn(apart, rows_f[...].astype(BF)).astype(BF)
    glv, gri, gcj, greal = split_part(iota((THREE, 1), 0), WLAT, 6)
    pk_g[...] = nn(one_hot(glv * HALF + gri * 6 + gcj, greal, TOK), own_g[...]).astype(BF)
    pl.semaphore_wait(barrier, len(greeted))
    send(pk_g, rl_g, C_GE, lon_ahead)
    for copy in small:
        copy.wait()
    s = lats_ref[0]
    t = lons_ref[0]
    late_row = s > WLAT // 2
    row_step = jnp.where(late_row, s - WLAT, s)
    col_step = t - WLON if late_col else t
    kvp[...] = jnp.zeros((8, D), F32)
    kvp[0:WLAT, 0:WLON] = valid_ref[...].astype(F32)

    def with_valid(sides, places):
        pieces, base = [], places[0][0]
        for at, end in places:
            pieces += [sides[at - base : end - base - 8], kvp[...]]
        return jnp.concatenate(pieces, 0).astype(BF)

    q_rows = jnp.concatenate([jnp.broadcast_to(q_ref[l : l + 1, :], (HEADS, D)) for l in range(2)], 0)
    row_head = iota((2 * HEADS, D), 0) % HEADS
    lane_head = lax.shift_right_logical(iota((2 * HEADS, D), 1), 5)
    q_rows = jnp.where(row_head == lane_head, q_rows.astype(F32), 0.0).astype(BF)
    lane_scale = lanes_of([etemp_ref[h] * SCALE for h in range(HEADS)] * 2, (1, 2 * HEADS), 1, 1)
    load_kvw.wait()
    load_lev.wait()
    load_eo = load(eo_hbm, eo)
    load_wo = load(wo_hbm, wo)
    wq_sem = lsem.at[len(loads)]
    for src, dst, width in ((0, 0, GW), (D, GW, GW), (GW, D, GW), (D + GW, D + GW, GW), (2 * D, 2 * D, D)):
        pltpu.make_async_copy(wq_hbm.at[:, pl.ds(src, width)], wq.at[:, pl.ds(dst, width)], wq_sem).start()
    filler = jnp.zeros((6, PADL - LEVELS, D), BF)

    def run_of(k):
        return 12 * (k % WLAT) + 6 * ((k // WLAT) ^ int(late_col))

    for k in range(2 * WLAT):
        block = jnp.concatenate([lev[run_of(k) : run_of(k) + 6], filler], 1)
        levp[6 * PADL * k : 6 * PADL * (k + 1), :] = block.reshape(6 * PADL, D)
    spread_row = iota((2 * HEADS, 2 * D), 0)
    spread = jnp.where(lax.shift_right_logical(iota((2 * HEADS, 2 * D), 1), 5) == spread_row, 1.0, 0.0).astype(BF)

    def encode_rows(low, high):
        rows, count = slice(low, high), (high - low) // PADL
        kv = nn(levp[rows, :], kvw[...])
        vals[rows, :] = kv[:, D:].astype(BF)
        sc = (nt(kv[:, :D].astype(BF), q_rows) * lane_scale).reshape(count, PADL, 2 * HEADS)
        sc = jnp.where(iota((count, PADL, 2 * HEADS), 1) < LEVELS, sc, NEG)
        e = jnp.exp(sc - jnp.max(sc, 1, keepdims=True))
        pm = e * (1.0 / jnp.sum(e, 1, keepdims=True))
        prob[rows, :] = pm.reshape(high - low, 2 * HEADS)

    def context_of(c):
        rows = slice(8 * PADL * c, 8 * PADL * (c + 1))
        w = nn(prob[rows, :].astype(BF), spread)
        wexp[rows, :] = w.astype(BF)
        v = vals[rows, :].astype(F32)
        for l in range(2):
            product = (w[:, l * D : (l + 1) * D] * v).reshape(8, 2, 8, D)
            product = (product[:, 0] + product[:, 1]).reshape(64, D)
            for j in range(4):
                part[4 * l + j, 64 * c : 64 * (c + 1), :] = product[:, 128 * j : 128 * (j + 1)]
        for l in range(2):
            for j in range(4):
                acc = part[4 * l + j, pl.ds(64 * c, 8, stride=8), :]
                for m in range(1, 8):
                    acc = acc + part[4 * l + j, pl.ds(64 * c + m, 8, stride=8), :]
                cback[l * HALF + 8 * c : l * HALF + 8 * (c + 1), 128 * j : 128 * (j + 1)] = acc

    def encoded_of(low, high):
        count = high - low
        context = jnp.concatenate([cback[low:high, :], cback[HALF + low : HALF + high, :]], 0)
        mixed = nn(context.astype(BF), eo[...])
        second = iota((2 * count, D), 0) >= count
        query = jnp.where(second, q_ref[1:2, :].astype(F32), q_ref[0:1, :].astype(F32))
        result = (query + mixed).astype(BF)
        for l in range(2):
            rows_f[l * HALF + low : l * HALF + high, :] = result[l * count : (l + 1) * count].astype(F32)
        return result

    encode_rows(0, 320)
    encode_rows(320, 640)
    for c in range(FIRST // 8):
        context_of(c)
    load_eo.wait()
    pk_e[:SIDES_1, :] = with_valid(nn(pack_first, encoded_of(0, FIRST)), PLACES[:3])
    send_sides(PLACES[:3], ahead[:3])
    encode_rows(640, 896)
    encode_rows(896, 1152)
    for c in range(FIRST // 8, HALF // 8):
        context_of(c)
    encoded_of(FIRST, HALF)
    own_e[...] = rows_f[...].astype(BF)
    pk_e[SIDES_1:, :] = with_valid(nn(pack_rest, own_e[...]), PLACES[3:])
    send_sides(PLACES[3:], ahead[3:])
    sel_own, sel_side = roll_matrices(row_step, col_step, late_col)
    near = nn(sel_own, own_e[...])
    two_own, two_side, two_far, two_edge_own, two_edge_side = two_step_matrices(
        row_step, col_step, False, late_col, split_token, own_index
    )
    near_g = nn(two_own, own_g[...])
    edge_g = nn(two_edge_own, own_g[...])
    tq = iota((1, GT), 1)
    for k in range(1, GRP):
        tq = jnp.where(iota((1, GT), 1) >= k * TOK, iota((1, GT), 1) - k * TOK, tq)
    qri = split_token(tq)[1]
    first_wrapped = 16 * WLAT - s
    window_row = jnp.where(late_row, (lat + 15) % 16, lat) * WLAT
    wk = jnp.where(window_row + ri >= first_wrapped, 1, 0)
    wqv = jnp.where(window_row + qri >= first_wrapped, 1, 0)
    kk = iota((TOK, GT), 0)
    fold[...] = jnp.where(kk == tq, 1.0, 0.0).astype(BF)
    fh = lax.shift_right_logical(iota((GW, GT), 0), 5)
    lane_t = iota((GW, GT), 1)
    hmask[...] = jnp.where((lane_t >= fh * TOK) & (lane_t < (fh + 1) * TOK), 1.0, 0.0).astype(BF)
    group_head = lax.shift_right_logical(iota((TOK, GW), 1), 5)
    eye = jnp.where(iota((GW, GW), 0) == iota((GW, GW), 1), 1.0, 0.0).astype(BF)
    scale_rows = [
        lanes_of([stemp_ref[g * GRP + h] * SCALE for h in range(GRP)], (1, GT), 1, TOK) for g in range(2)
    ]
    n = iota((256, 1), 0)
    bit = lambda shift, mask: lax.shift_right_logical(n, shift) & mask
    wrow = bit(7, 1) * 256 + bit(4, 3) * 64 + core * 32 + bit(1, 7) * 4 + bit(6, 1) * 2 + (n & 1)
    pick = one_hot(wrow, n >= 0, D)

    back_own, back_side, back_far, bedge_own, bedge_side = two_step_matrices(
        -row_step, -col_step, True, not late_col, own_place, window_index
    )
    pltpu.make_async_copy(wq_hbm, wq, wq_sem).wait()
    arrived(C_GE)
    sn_g[...] = (edge_g + nn(two_edge_side, rl_g[...])).astype(BF)
    send_lat(sn_g, rn_g, C_GN, south, north)
    near_g = near_g + nn(two_side, rl_g[...])
    arrived(C_EE)
    beside = rl_e[THREE_DIAG - 8 : THREE_DIAG, :].astype(F32) if late_col else kvp[...]
    end = THREE_AT if late_col else SIDES
    valid_2 = jnp.where(late_row, rl_e[end - 8 : end, :].astype(F32), beside)
    lane = iota((TOK, 128), 1)
    valid_row = jnp.zeros((TOK, 128), F32)
    for r in range(WLAT):
        valid_row = jnp.where(ri == r, valid_2[r : r + 1, :128], valid_row)
    valid_k = jnp.sum(jnp.where(lane == cj, valid_row, 0.0), 1, keepdims=True)
    ok = (wk == wqv) & ((valid_k > 0.5) | (kk == tq))
    bias[...] = jnp.where(ok, 0.0, NEG)
    rolled = near + nn(sel_side, rl_e[...])

    mean = jnp.mean(rolled, 1, keepdims=True)
    centered = rolled - mean
    inv = lax.rsqrt(jnp.mean(centered * centered, 1, keepdims=True) + EPS)
    unit_v = centered * inv
    unit[...] = unit_v
    normed[...] = unit_v.astype(BF)
    send(normed, m_normed, C_TN, mate)
    qkv[...] = nn(normed[...], wq[...]).astype(BF)
    scores, values_t, turned = [], [], []
    for g in range(2):
        qg = qkv[:, g * D : g * D + GW]
        for h in range(GRP):
            qs[g, h * TOK : (h + 1) * TOK, :] = jnp.where(group_head == h, qg, jnp.zeros_like(qg))
        scores.append(nt(qkv[:, g * D + GW : (g + 1) * D], qs[g]))
    for g in range(2):
        values_t.append(nt(eye, qkv[:, 2 * D + g * GW : 2 * D + (g + 1) * GW]).astype(BF))
    for g in range(2):
        st = scores[g] * scale_rows[g] + bias[...]
        e = jnp.exp(st - jnp.max(st, 0, keepdims=True))
        p = e * (1.0 / jnp.sum(e, 0, keepdims=True))
        pt[g] = p
        p16[g] = p.astype(BF)
        turned.append(nn(values_t[g], p16[g]).astype(BF) * hmask[...])
    for g in range(2):
        ctx[:, g * GW : (g + 1) * GW] = nt(fold[...], turned[g]).astype(BF)
    send(ctx, m_ctx, C_TC, mate)
    load_wo.wait()
    att[...] = nn(ctx[...], wo[...]).astype(BF)
    pk_a[...] = nn(pack_back, att[...]).astype(BF)
    send(pk_a, rl_a, C_AW, lon_back)
    arrived(C_GN)
    rgrad[...] = (near_g + nn(two_far, rn_g[...])).astype(BF)
    send(rgrad, m_rgrad, C_TR, mate)
    cgrad = nt(rgrad[...], wo[...]).astype(BF)
    for g in range(2):
        piece = cgrad[:, g * GW : (g + 1) * GW]
        for h in range(GRP):
            cgs[g, h * TOK : (h + 1) * TOK, :] = jnp.where(group_head == h, piece, jnp.zeros_like(piece))
    for g in range(2):
        qgrad[:, 2 * D + g * GW : 2 * D + (g + 1) * GW] = nn(p16[g], cgs[g]).astype(BF)
    third = [pl.ds(k * D, D) for k in range(3)]
    send(qgrad.at[:, third[2]], m_qgrad.at[:, third[2]], C_TV, mate)

    def scores_back(g):
        p = pt[g]
        dp = nt(qkv[:, 2 * D + g * GW : 2 * D + (g + 1) * GW], cgs[g])
        ds = p * (dp - jnp.sum(p * dp, 0, keepdims=True)) * scale_rows[g]
        ds16 = ds.astype(BF)
        k_t = nt(eye, qkv[:, g * D + GW : (g + 1) * D]).astype(BF)
        q_t = nn(k_t, ds16).astype(BF) * hmask[...]
        qgrad[:, g * D : g * D + GW] = nt(fold[...], q_t).astype(BF)
        qgrad[:, g * D + GW : (g + 1) * D] = nn(ds16, qs[g]).astype(BF)
        send(qgrad.at[:, third[g]], m_qgrad.at[:, third[g]], C_TQ0 + g, mate)

    def picked(left, m_left):
        return nt(pick, left[...]).astype(BF), nt(pick, m_left[...]).astype(BF)

    def chip_sum(lefts, right, m_right):
        total = nn(lefts[0], right) + nn(lefts[1], m_right)
        return total.astype(BF).reshape(NY, NX, 16, right.shape[1])

    def share(k_set, low_a, width_a, low_b, width_b):
        send_a, send_b, r1a, r1b = (early, late)[k_set][:4]
        a, b = pl.ds(low_a, width_a), pl.ds(low_b, width_b)
        for k in range(1, NY):
            src = send_a.at[(y + k) % NY, :, :, a]
            send(src, r1a.at[k - 1, :, :, a], C_1 + 2 * k_set, y_peers[k - 1], r1a)
        for k in range(1, NX):
            src = send_b.at[:, (x + k) % NX, :, b]
            send(src, r1b.at[k - 1, :, :, b], C_1 + 2 * k_set + 1, x_peers[k - 1], r1b)

    def second_stage(k_set):
        send_a, send_b, r1a, r1b, s2a, s2b, r2a, r2b = (early, late)[k_set]
        arrived(C_1 + 2 * k_set)
        arrived(C_1 + 2 * k_set + 1)
        sum_a = send_a[y].astype(F32)
        sum_b = send_b[:, x].astype(F32)
        for k in range(3):
            sum_a = sum_a + r1a[k].astype(F32)
            sum_b = sum_b + r1b[k].astype(F32)
        s2a[...] = sum_a.astype(BF)
        s2b[...] = sum_b.astype(BF)
        for k in range(1, NX):
            send(s2a.at[(x + k) % NX], r2a.at[k - 1], C_2 + 2 * k_set, x_peers[k - 1], r2a)
        for k in range(1, NY):
            send(s2b.at[(y + k) % NY], r2b.at[k - 1], C_2 + 2 * k_set + 1, y_peers[k - 1], r2b)

    def second_sums(k_set):
        s2a, s2b, r2a, r2b = (early, late)[k_set][4:]
        arrived(C_2 + 2 * k_set)
        arrived(C_2 + 2 * k_set + 1)
        sum_a = s2a[x].astype(F32)
        sum_b = s2b[y].astype(F32)
        for k in range(3):
            sum_a = sum_a + r2a[k].astype(F32)
            sum_b = sum_b + r2b[k].astype(F32)
        return sum_a, sum_b

    scores_back(0)
    arrived(C_TC)
    arrived(C_TR)
    g_out = chip_sum(picked(ctx, m_ctx), rgrad[...], m_rgrad[...])
    early[0][:, :, :, 256:] = g_out[:, :, :, :256]
    early[1][:, :, :, 256:] = g_out[:, :, :, 256:]
    share(0, 256, 256, 256, 256)
    arrived(C_TN)
    arrived(C_TV)
    lefts = picked(normed, m_normed)
    g_val = chip_sum(lefts, qgrad[:, 2 * D :], m_qgrad[:, 2 * D :])
    early[0][:, :, :, :256] = g_val[:, :, :, :256]
    early[1][:, :, :, :256] = g_val[:, :, :, 256:]
    share(0, 0, 256, 0, 256)
    scores_back(1)

    def sum_qk(g):
        arrived(C_TQ0 + g)
        return chip_sum(lefts, qgrad[:, g * D : (g + 1) * D], m_qgrad[:, g * D : (g + 1) * D])

    g_qk = sum_qk(0)
    late[0][:, :, :, :256] = g_qk[:, :, :, :256]
    late[1][:, :, :, :256] = g_qk[:, :, :, 256:]
    share(1, 0, 256, 0, 256)
    ugrad = nt(qgrad[...], wq[...])
    u = unit[...]
    xgrad = inv * (
        ugrad - jnp.mean(ugrad, 1, keepdims=True) - u * jnp.mean(ugrad * u, 1, keepdims=True)
    )
    xg[...] = xgrad.astype(BF)
    pk_x[...] = nn(pack_back, xg[...]).astype(BF)
    send(pk_x, rl_x, C_XW, lon_back)
    g_qk = sum_qk(1)
    late[0][:, :, :, 256:] = g_qk[:, :, :, :128]
    late[1][:, :, :, 256:] = g_qk[:, :, :, 128:]
    share(1, 256, 128, 256, 384)
    near_x = own_g[...].astype(F32) + nn(back_own, xg[...])
    key_q = nt(q_rows, kvw[:, :D]).astype(BF)
    edge_x = nn(bedge_own, xg[...])
    arrived(C_XW)
    sn_x[...] = (edge_x + nn(bedge_side, rl_x[...])).astype(BF)
    send_lat(sn_x, rn_x, C_XS, north, south)
    near_x = near_x + nn(back_side, rl_x[...])
    second_stage(0)
    second_stage(1)
    arrived(C_XS)
    arrived(C_AW)
    sn_a[...] = (nn(bedge_own, att[...]) + nn(bedge_side, rl_a[...])).astype(BF)
    send_lat(sn_a, rn_a, C_AS, north, south)
    egrad = (near_x + nn(back_far, rn_x[...])).astype(BF)

    cback[...] = nt(egrad, eo[...]).astype(BF).astype(F32)

    def products(c, carry):
        first = cback[pl.ds(pl.multiple_of(8 * c, 8), 8), :]
        second = cback[pl.ds(pl.multiple_of(HALF + 8 * c, 8), 8), :]
        for p in range(8):
            rows = pl.ds(pl.multiple_of(8 * PADL * c + p * PADL, PADL), PADL)
            c0, c1 = first[p : p + 1, :], second[p : p + 1, :]
            v = vals[rows, :].astype(F32)
            prod[rows, :D] = (c0 * v).astype(BF)
            prod[rows, D:] = (c1 * v).astype(BF)
            vgrad[rows, :] = (wexp[rows, :D].astype(F32) * c0 + wexp[rows, D:].astype(F32) * c1).astype(BF)
        return carry

    lax.fori_loop(0, HALF // 8, products, 0)

    sums = [*second_sums(1), *second_sums(0)]
    chunks = [v[:, 128 * i : 128 * (i + 1)] for v in sums for i in range(v.shape[1] // 128)]
    for i, value in enumerate(chunks):
        s3f[i % 2, pl.ds(i // 2, 16, stride=8), :] = value
    for k in range(NZ):
        for h in range(2):
            s3[k, :, 128 * h : 128 * (h + 1)] = s3f[h, 16 * k : 16 * (k + 1), :].astype(BF)
    for k in range(1, NZ):
        send(s3.at[(z + k) % NZ], r3.at[k - 1], C_3, z_peers[k - 1], r3)

    for c in range(ROWS // CHUNK):
        rows = slice(c * CHUNK, (c + 1) * CHUNK)
        pg = nt(prod[rows, :], spread).reshape(CHUNK // PADL, PADL, 2 * HEADS)
        pm = prob[rows, :].reshape(CHUNK // PADL, PADL, 2 * HEADS)
        sg = pm * (pg - jnp.sum(pm * pg, 1, keepdims=True))
        prob[rows, :] = sg.reshape(CHUNK, 2 * HEADS) * lane_scale

    def level_grads(c):
        rows = slice(c * CHUNK, (c + 1) * CHUNK)
        lg = nt(vgrad[rows, :], kvw[:, D:]) + nn(prob[rows, :].astype(BF), key_q)
        lg = lg.astype(BF).reshape(CHUNK // PADL, PADL, D)
        for k in range(4):
            lg_v[run_of(4 * c + k) : run_of(4 * c + k) + 6] = lg[6 * k : 6 * (k + 1), :LEVELS, :]

    for c in range(3):
        level_grads(c)
    stores = [pltpu.make_async_copy(lg_v, lg_hbm, lsem.at[len(loads) + 1])]
    stores[-1].start()
    arrived(C_AS)
    added = nn(back_own, att[...]) + nn(back_side, rl_a[...]) + nn(back_far, rn_a[...])
    out16 = (own_e[...].astype(F32) + added).astype(BF)
    u_row = iota((TOK, 1), 0)
    u_patch = lax.shift_right_logical(u_row, 1)
    u_lat = lax.shift_right_logical(u_patch * 171, 11)
    together = one_hot(own_index(u_row & 1, u_lat, u_patch - u_lat * WLON), u_row >= 0, TOK)
    rows_f[...] = nn(together, out16)
    for p in range(HALF):
        out_v[p] = rows_f[2 * p : 2 * p + 2, :].astype(BF)
    stores.append(pltpu.make_async_copy(out_v, out_hbm, lsem.at[len(loads) + 2]))
    stores[-1].start()

    arrived(C_3)
    factor = GRAD_GAIN * (2 * 96 * 192) ** (-0.5)
    for h in range(2):
        total = s3f[h, pl.ds(pl.multiple_of(16 * z, 16), 16), :]
        for k in range(NZ - 1):
            total = total + r3[k, :, 128 * h : 128 * (h + 1)].astype(F32)
        total = total * factor
        for b in range(2):
            for j in range(8):
                piece = total[8 * b + j : 8 * b + j + 1, :]
                place = PIECES[2 * j + h]
                if place < 12:
                    gq_ref[12 * b + place : 12 * b + place + 1, :] = piece
                else:
                    go_ref[4 * b + place - 12 : 4 * b + place - 11, :] = piece
    for i, (src, dst) in enumerate(((gq_ref, gq_hbm), (go_ref, go_hbm))):
        stores.append(pltpu.make_async_copy(src, dst, lsem.at[len(loads) + 3 + i]))
        stores[-1].start()
    for index in landings:
        whole(index).wait_send()
    for copy in stores:
        copy.wait()


def deliver(a, b, c, d, a_out, b_out, c_out, d_out, sems):
    pairs = ((a, a_out), (b, b_out), (c, c_out), (d, d_out))
    copies = [pltpu.make_async_copy(src, dst, sems.at[i]) for i, (src, dst) in enumerate(pairs)]
    for copy in copies:
        copy.start()
    for copy in copies:
        copy.wait()


def local(levels_in, latent_queries, enc_kv, enc_out, enc_temp, w_qkv, w_out, swin_temp, lat_shift, lon_shift, key_valid, output_grad):
    hbm = pl.BlockSpec(memory_space=pl.ANY)
    V = pltpu.VMEM
    block = lambda rows: V((rows, D), BF)
    scratch = [
        V((HALF, LEVELS, D), BF), V((D, 2 * D), BF), V((D, D), BF), V((D, 3 * D), BF), V((D, D), BF), V((HALF, 2, D), BF),
        V((2, D), BF), pltpu.SMEM((HEADS,), F32), pltpu.SMEM((HEADS,), F32), pltpu.SMEM((1,), jnp.int32),
        pltpu.SMEM((1,), jnp.int32), V((WLAT, WLON), jnp.int32),
        V((ROWS, D), BF),
        V((ROWS, D), BF),
        V((ROWS, 2 * HEADS), F32),
        V((ROWS, 2 * D), BF),
        V((ROWS, 2 * D), BF),
        V((ROWS, D), BF),
        V((8, 8 * HALF, 128), F32),
        V((TOK, D), F32),
        V((TOK, D), F32),
        V((8, D), F32),
        V((HALF, 2, D), BF),
        V((HALF, LEVELS, D), BF),
        V((24, 128), F32), V((8, 128), F32),
    ]
    scratch += [block(TOK), block(SIDES), block(SIDES)]
    for _ in range(3):
        scratch += [block(TOK), block(THREE), block(THREE), block(BOTH), block(BOTH)]
    scratch += [
        V((TOK, D), F32), V((TOK, 3 * D), BF), block(TOK), block(TOK), block(TOK), V((TOK, 3 * D), BF),
        block(TOK), block(TOK), block(TOK), V((TOK, 3 * D), BF),
        V((2, GT, GW), BF), V((2, GT, GW), BF), V((2, TOK, GT), F32), V((2, TOK, GT), BF),
        V((TOK, GT), F32), V((GW, GT), BF), V((TOK, GT), BF),
        *(
            tuple(V((*lead, 16, w), BF) for lead in ((NY, NX), (3, NX), (NX,), (3,)) for w in pair)
            for pair in WIDTHS
        ),
        V((2, 128, 128), F32), V((NZ, 16, 256), BF), V((NZ - 1, 16, 256), BF),
        pltpu.SemaphoreType.DMA((16,)),
        pltpu.SemaphoreType.DMA((N_COPY,)),
        pltpu.SemaphoreType.DMA((N_COPY,)),
    ]
    lev = jnp.transpose(levels_in, (1, 2, 0, 3)).reshape(HALF, LEVELS, D)
    og = jnp.transpose(output_grad, (1, 2, 0, 3)).reshape(HALF, 2, D)
    shapes = (
        jax.ShapeDtypeStruct((HALF, 2, D), BF),
        jax.ShapeDtypeStruct((HALF, LEVELS, D), BF),
        jax.ShapeDtypeStruct((24, 128), F32),
        jax.ShapeDtypeStruct((8, 128), F32),
    )

    def run(late_col):
        return pl.pallas_call(
            functools.partial(kernel, late_col),
            out_shape=shapes,
            in_specs=[hbm] * 12,
            out_specs=(hbm,) * 4,
            scratch_shapes=scratch,
            compiler_params=pltpu.CompilerParams(
                collective_id=int(late_col), has_side_effects=True, vmem_limit_bytes=48 * 1024 * 1024
            ),
        )

    parts = lax.cond(
        lon_shift[0] > WLON // 2, run(True), run(False),
        lev, latent_queries, enc_kv, enc_out, enc_temp, w_qkv, w_out, swin_temp, lat_shift, lon_shift, key_valid, og,
    )
    out, lg, gq, go = pl.pallas_call(
        deliver,
        out_shape=shapes,
        in_specs=[hbm] * 4,
        out_specs=(hbm,) * 4,
        scratch_shapes=[pltpu.SemaphoreType.DMA((4,))],
    )(*parts)
    out = jnp.transpose(out.reshape(WLAT, WLON, 2, D), (2, 0, 1, 3))
    lg = jnp.transpose(lg.reshape(WLAT, WLON, LEVELS, D), (2, 0, 1, 3))
    return out, lg, gq.reshape(-1), go.reshape(-1)


def solution(mesh):
    return jax.shard_map(
        local,
        mesh=mesh,
        in_specs=(
            P(None, "lat", "lon", None), P(), P(), P(), P(), P(), P(), P(), P(), P(),
            P("lat", "lon"),
            P(None, "lat", "lon", None),
        ),
        out_specs=(
            P(None, "lat", "lon", None),
            P(None, "lat", "lon", None),
            P(("lat", "lon")),
            P(("lat", "lon")),
        ),
        check_vma=False,
    )
```
